128 devices in a mesh: dp: 32 (over y, x, z_lo), sp: 4 (over z_hi, core).
Axes of the slice: x: 4, y: 4, z: 4 (z_hi: 2, z_lo: 2; z = z_hi * 2 + z_lo), core: 2. Of those that a mesh axis runs over, the one named last changes fastest.
Arguments:
- queries: bfloat16 [32, 1024, 2048], P('dp', 'sp'), may hold values from -80 to 80
- keys: bfloat16 [32, 1024, 512], P('dp', 'sp'), may hold values from -16 to 16
- values: bfloat16 [32, 1024, 512], P('dp', 'sp'), may hold values from -6 to 6
- cotangent: bfloat16 [32, 1024, 2048], P('dp', 'sp'), may hold values from -6 to 6
- doc_ids: int32 [32, 1024], P('dp', 'sp'), may hold values from 0 to 7, as said below
- partners: int32 [16, 32], P(None, 'dp'), may hold values from 0 to 31, as said below
- swap_slots: int32 [32, 4, 16], P('dp', 'sp'), may hold values from 0 to 31, as said below
Outputs:
- attended: bfloat16 [32, 1024, 2048], P('dp', 'sp')
- grad_queries: bfloat16 [32, 1024, 2048], P('dp', 'sp')
- grad_keys: bfloat16 [32, 1024, 512], P('dp', 'sp')
- grad_values: bfloat16 [32, 1024, 512], P('dp', 'sp')
The draws below stay inside these ranges and needn't reach their ends.
Inputs may be any that keep to these rules, and one draw needn't show every extreme that they name: Each row t is a pairing of the groups: partners[t, partners[t, i]] = i and partners[t, i] != i; no two rounds give a group the same partner. `swap_slots`: for each group and sp index the 16 block numbers are distinct. `doc_ids`: along each group's slice the ids start at 0, never fall, rise only at positions that are multiples of 8, and every id of 0 to 7 occurs.
All inputs are finite; a program needn't handle non-finite values.
Results may differ from the reference program's by a relative error of at most 0.008.
Values may be sent and summed in bfloat16 or wider, within the bound.
No kernel may reach another device: no remote copies, remote signals or barrier semaphores. Data moves between devices by JAX's collectives and lax.ppermute only.
A program may use at most 128 MiB of HBM per device.

```python
import math
import jax
import jax.numpy as jnp
from jax import lax

QUERY_HEADS = 16
KEY_VALUE_HEADS = 4
HEAD_SIZE = 128
TOK_DEV = 256
BLOCK = 8
NDOC = 8
ROUNDS = 16
SLICE_POSITIONS = 1024
N_DP = 32
N_SP = 4


def draw_queries(key, part):
    key = jax.random.fold_in(key, 3)
    leading_key, trailing_key = jax.random.split(key)
    dispersal = jnp.exp(jax.random.uniform(trailing_key, (N_DP, SLICE_POSITIONS, QUERY_HEADS, 1), jnp.float32, math.log(0.4), math.log(2.5)))
    sampled_items = jnp.clip(jax.random.normal(leading_key, (N_DP, SLICE_POSITIONS, QUERY_HEADS, HEAD_SIZE), jnp.float32), -5.0, 5.0) * dispersal
    return sampled_items.reshape(N_DP, SLICE_POSITIONS, QUERY_HEADS * HEAD_SIZE).astype(jnp.bfloat16)


def draw_keys(key, part):
    key = jax.random.fold_in(key, 5)
    leading_key, trailing_key = jax.random.split(key)
    dispersal = jnp.exp(jax.random.uniform(trailing_key, (N_DP, SLICE_POSITIONS, KEY_VALUE_HEADS, 1), jnp.float32, math.log(0.4), math.log(2.5)))
    sampled_items = jnp.clip(jax.random.normal(leading_key, (N_DP, SLICE_POSITIONS, KEY_VALUE_HEADS, HEAD_SIZE), jnp.float32), -5.0, 5.0) * dispersal
    return sampled_items.reshape(N_DP, SLICE_POSITIONS, KEY_VALUE_HEADS * HEAD_SIZE).astype(jnp.bfloat16)


def draw_doc_ids(key, part):
    key = jax.random.fold_in(key, 7)
    unit_count = SLICE_POSITIONS // 8
    scores = jax.random.randint(key, (N_DP, unit_count - 1), 0, 1 << 20) * (unit_count - 1) + jnp.arange(unit_count - 1, dtype=jnp.int32)[None, :]
    ranking = jnp.argsort(scores, axis=1)
    boundary = ranking[:, :NDOC - 1].astype(jnp.int32) + 1
    unit_pos = jnp.arange(unit_count, dtype=jnp.int32)
    doc_numbers = jnp.sum((boundary[:, None, :] <= unit_pos[None, :, None]).astype(jnp.int32), axis=-1)
    return jnp.repeat(doc_numbers, 8, axis=1).astype(jnp.int32)


def draw_partners(key, part):
    key = jax.random.fold_in(key, 11)
    leading_key, trailing_key = jax.random.split(key)
    labels = jax.random.permutation(leading_key, N_DP).astype(jnp.int32)
    chosen = jax.random.permutation(trailing_key, N_DP - 1)[:ROUNDS].astype(jnp.int32)
    seat_ids = jnp.arange(N_DP, dtype=jnp.int32)
    fixed_seat = N_DP - 1
    mate_seat = jnp.where(seat_ids[None, :] == fixed_seat, chosen[:, None], jnp.where(seat_ids[None, :] == chosen[:, None], fixed_seat, jnp.mod(2 * chosen[:, None] - seat_ids[None, :], fixed_seat)))
    mapped = labels[mate_seat]
    return jnp.zeros((ROUNDS, N_DP), jnp.int32).at[:, labels].set(mapped)


def draw_swap_slots(key, part):
    key = jax.random.fold_in(key, 13)
    block_count = TOK_DEV // BLOCK
    scores = jax.random.randint(key, (N_DP, N_SP, block_count), 0, 1 << 20) * block_count + jnp.arange(block_count, dtype=jnp.int32)
    ranking = jnp.argsort(scores, axis=-1)
    return ranking[:, :, :ROUNDS].astype(jnp.int32)


def shard_levels(rng, extent, shards, smallest, largest):
    loudness = 1.0
    for dim, parts in shards:
        steps = jax.random.uniform(jax.random.fold_in(jax.random.fold_in(rng, 6), dim), (parts,), jnp.float32, smallest / len(shards), largest / len(shards))
        loudness = loudness * jnp.repeat(jnp.exp(steps), extent[dim] // parts).reshape((-1,) + (1,) * (len(extent) - 1 - dim))
    return loudness


def scatter_about(rng, shape, deviation, bound, shards=(), held_as=jnp.bfloat16):
    result = jax.random.normal(rng, shape, jnp.float32) * deviation
    if len(shards) > 0:
        result = shard_levels(rng, shape, shards, -0.22, 0.18) * result
    return jnp.clip(result, min=-bound, max=bound).astype(held_as)


def setup_inputs(seed: int = 0) -> dict:
    seeds = jax.random.split(jax.random.key(seed), 8)
    queries = draw_queries(jax.random.fold_in(seeds[7], 71), 0)
    keys = draw_keys(jax.random.fold_in(seeds[7], 71), 0)
    values = scatter_about(seeds[2], (N_DP, SLICE_POSITIONS, KEY_VALUE_HEADS * HEAD_SIZE), 1.0, 6.0, ((0, 32), (1, 4)))
    cotangent = scatter_about(seeds[3], (N_DP, SLICE_POSITIONS, QUERY_HEADS * HEAD_SIZE), 1.0, 6.0, ((0, 32), (1, 4)))
    doc_ids = draw_doc_ids(jax.random.fold_in(seeds[7], 71), 0)
    partners = draw_partners(jax.random.fold_in(seeds[7], 71), 0)
    swap_slots = draw_swap_slots(jax.random.fold_in(seeds[7], 71), 0)
    return {"queries": queries, "keys": keys, "values": values, "cotangent": cotangent, "doc_ids": doc_ids, "partners": partners, "swap_slots": swap_slots}


def repack(array, partners, swap_slots):
    block_count = TOK_DEV // BLOCK
    columns = array.shape[-1]
    repeated_tiling = array.reshape(N_DP, N_SP, block_count, BLOCK, columns)
    shape_all = swap_slots.shape
    group_ids = jnp.broadcast_to(jnp.arange(N_DP, dtype=jnp.int32)[:, None, None], shape_all)
    rank_ids = jnp.broadcast_to(jnp.arange(N_SP, dtype=jnp.int32)[None, :, None], shape_all)
    round_ids = jnp.broadcast_to(jnp.arange(ROUNDS, dtype=jnp.int32)[None, None, :], shape_all)
    mate_ids = jnp.broadcast_to(jnp.transpose(partners)[:, None, :], shape_all).astype(jnp.int32)
    source_slot = swap_slots[mate_ids, rank_ids, round_ids].astype(jnp.int32)
    moved = repeated_tiling[mate_ids, rank_ids, source_slot]
    repeated_tiling = repeated_tiling.at[group_ids, rank_ids, swap_slots.astype(jnp.int32)].set(moved)
    return repeated_tiling.reshape(array.shape)


def attend_group(items):
    query_row_set, key_row_set, value_row_set, gradient_row_set, doc_row = items
    group_sharing = QUERY_HEADS // KEY_VALUE_HEADS
    query_lattice = query_row_set.astype(jnp.float32).reshape(SLICE_POSITIONS, KEY_VALUE_HEADS, group_sharing, HEAD_SIZE)
    key_lattice = key_row_set.astype(jnp.float32).reshape(SLICE_POSITIONS, KEY_VALUE_HEADS, HEAD_SIZE)
    value_lattice = value_row_set.astype(jnp.float32).reshape(SLICE_POSITIONS, KEY_VALUE_HEADS, HEAD_SIZE)
    gradient_lattice = gradient_row_set.astype(jnp.float32).reshape(SLICE_POSITIONS, KEY_VALUE_HEADS, group_sharing, HEAD_SIZE)
    factor = HEAD_SIZE ** -0.5
    logits = jnp.einsum("qkge,pke->kgqp", query_lattice, key_lattice) * factor
    position = jnp.arange(SLICE_POSITIONS, dtype=jnp.int32)
    allowed = (doc_row[:, None] == doc_row[None, :]) & (position[None, :] <= position[:, None])
    logits = jnp.where(allowed, logits, -jnp.inf)
    maximum = jnp.max(logits, axis=-1, keepdims=True)
    raised = jnp.exp(logits - maximum)
    row_total = jnp.sum(raised, axis=-1, keepdims=True)
    weights = raised / row_total
    weights_low = lax.optimization_barrier(weights.astype(jnp.bfloat16)).astype(jnp.float32)
    attended = jnp.einsum("kgqp,pke->qkge", weights_low, value_lattice).astype(jnp.bfloat16)
    grad_weights = jnp.einsum("qkge,pke->kgqp", gradient_lattice, value_lattice)
    inner_sum = jnp.sum(weights * grad_weights, axis=-1, keepdims=True)
    grad_logits = lax.optimization_barrier((weights * (grad_weights - inner_sum)).astype(jnp.bfloat16)).astype(jnp.float32)
    grad_query = (jnp.einsum("kgqp,pke->qkge", grad_logits, key_lattice) * factor).astype(jnp.bfloat16)
    key_gradient = (jnp.einsum("kgqp,qkge->pke", grad_logits, query_lattice) * factor).astype(jnp.bfloat16)
    value_gradient = jnp.einsum("kgqp,qkge->pke", weights_low, gradient_lattice).astype(jnp.bfloat16)
    return (attended.reshape(SLICE_POSITIONS, QUERY_HEADS * HEAD_SIZE), grad_query.reshape(SLICE_POSITIONS, QUERY_HEADS * HEAD_SIZE),
            key_gradient.reshape(SLICE_POSITIONS, KEY_VALUE_HEADS * HEAD_SIZE), value_gradient.reshape(SLICE_POSITIONS, KEY_VALUE_HEADS * HEAD_SIZE))


def reference(queries, keys, values, cotangent, doc_ids, partners, swap_slots):
    packed_q = repack(queries, partners, swap_slots)
    packed_k = repack(keys, partners, swap_slots)
    packed_v = repack(values, partners, swap_slots)
    packed_g = repack(cotangent, partners, swap_slots)
    results = lax.map(attend_group, (packed_q, packed_k, packed_v, packed_g, doc_ids))
    return (repack(results[0], partners, swap_slots), repack(results[1], partners, swap_slots),
            repack(results[2], partners, swap_slots), repack(results[3], partners, swap_slots))
```

```python
import jax
import jax.numpy as jnp
from jax import lax
from jax.experimental import pallas as pl
from jax.experimental.pallas import tpu as pltpu
from jax.sharding import PartitionSpec as P

KEY_VALUE_HEADS = 4
SHARED = 4
HEAD_SIZE = 128
BLOCK = 8
ROUNDS = 16
ROWS = 256
HALF = ROUNDS * BLOCK
GROUPS = 32
RANKS = 4
WIDE = SHARED * HEAD_SIZE
PAIR = 2 * HEAD_SIZE
BUNDLE = WIDE + PAIR
META = 384
FACTOR = HEAD_SIZE ** (-0.5)
EXP2_FACTOR = FACTOR * 1.4426950408889634
MASKED = -1e30
BF16 = jnp.bfloat16
F32 = jnp.float32

SMEM = pl.BlockSpec(memory_space=pltpu.SMEM)
PARAMS = pltpu.CompilerParams(vmem_limit_bytes=56 * 1024 * 1024)


def iota(shape, axis):
    return lax.broadcasted_iota(jnp.int32, shape, axis)


def onehot(hit):
    return jnp.where(hit, 1.0, 0.0).astype(BF16)


def pick(matrix, rows):
    return jnp.dot(matrix, rows, preferred_element_type=F32).astype(BF16)


def position(axis, count=ROWS):
    return iota((count, 1) if axis == 0 else (1, count), axis)


def sent_row(mate, slot):
    place = position(0)
    block = jnp.zeros_like(place)
    for t in range(ROUNDS):
        block = jnp.where(place >> 3 == mate[t], slot[t], block)
    return block * BLOCK + (place & 7)


def landed_row(mate, slot):
    place = position(0)
    group = jnp.full_like(place, -1)
    for t in range(ROUNDS):
        group = jnp.where(place >> 3 == slot[t], mate[t], group)
    return jnp.where(group >= 0, group * BLOCK + (place & 7), -1)


def packed_row(slot, axis):
    place = position(axis)
    block = place >> 3
    lower = jnp.zeros_like(place)
    turn = jnp.full_like(place, -1)
    for t in range(ROUNDS):
        lower = lower + (block > slot[t]).astype(jnp.int32)
        turn = jnp.where(block == slot[t], t, turn)
    return jnp.where(turn >= 0, HALF + turn * BLOCK, (block - lower) * BLOCK) + (place & 7)


def turn_row(mate):
    place = position(0, HALF)
    group = jnp.zeros_like(place)
    for t in range(ROUNDS):
        group = jnp.where(place >> 3 == t, mate[t], group)
    return group * BLOCK + (place & 7)


def sent_turn(mate):
    place = position(0)
    turn = jnp.zeros_like(place)
    for t in range(ROUNDS):
        turn = jnp.where(place >> 3 == mate[t], t, turn)
    return turn * BLOCK + (place & 7)


def scalars(ref, first, count):
    return [ref[first + t] for t in range(count)]


def lanes(width):
    return iota((1, width), 1)


def outgoing_kernel(mate_ref, slot_ref, q_ref, k_ref, v_ref, g_ref, first_ref, second_ref, stay_ref, choose, keep):
    @pl.when(pl.program_id(0) == 0)
    def _():
        mate, slot = scalars(mate_ref, 0, ROUNDS), scalars(slot_ref, 0, ROUNDS)
        choose[...] = onehot(sent_row(mate, slot) == lanes(ROWS))
        keep[...] = onehot(packed_row(slot, 1) == position(0, HALF))

    pairs = jnp.concatenate([k_ref[...], v_ref[...]], axis=1)
    first_ref[...] = pick(choose[...], jnp.concatenate([q_ref[...], pairs], axis=1))
    second_ref[...] = pick(choose[...], g_ref[...])
    stay_ref[...] = pick(keep[...], pairs)


def outgoing(mate, slot, q, k, v, g):
    return pl.pallas_call(
        outgoing_kernel,
        grid=(KEY_VALUE_HEADS,),
        in_specs=[
            SMEM,
            SMEM,
            pl.BlockSpec((ROWS, WIDE), lambda h: (0, h)),
            pl.BlockSpec((ROWS, HEAD_SIZE), lambda h: (0, h)),
            pl.BlockSpec((ROWS, HEAD_SIZE), lambda h: (0, h)),
            pl.BlockSpec((ROWS, WIDE), lambda h: (0, h)),
        ],
        out_specs=[
            pl.BlockSpec((ROWS, BUNDLE), lambda h: (0, h)),
            pl.BlockSpec((ROWS, WIDE), lambda h: (0, h)),
            pl.BlockSpec((HALF, PAIR), lambda h: (0, h)),
        ],
        out_shape=[
            jax.ShapeDtypeStruct((ROWS, KEY_VALUE_HEADS * BUNDLE), BF16),
            jax.ShapeDtypeStruct((ROWS, KEY_VALUE_HEADS * WIDE), BF16),
            jax.ShapeDtypeStruct((HALF, KEY_VALUE_HEADS * PAIR), BF16),
        ],
        scratch_shapes=[pltpu.VMEM((ROWS, ROWS), BF16), pltpu.VMEM((HALF, ROWS), BF16)],
        compiler_params=PARAMS,
        cost_estimate=pl.CostEstimate(flops=10**9, bytes_accessed=5 * 10**6, transcendentals=0),
        name="outgoing",
    )(mate, slot, q, k, v, g)


def traded_pairs_kernel(mate_ref, landed_ref, out_ref, choose):
    @pl.when(pl.program_id(0) == 0)
    def _():
        choose[...] = onehot(turn_row(scalars(mate_ref, 0, ROUNDS)) == lanes(ROWS))

    out_ref[...] = pick(choose[...], landed_ref[...])


def traded_pairs(mate, landed):
    return pl.pallas_call(
        traded_pairs_kernel,
        grid=(KEY_VALUE_HEADS,),
        in_specs=[SMEM, pl.BlockSpec((ROWS, PAIR), lambda h: (0, 3 * h + 2))],
        out_specs=pl.BlockSpec((HALF, PAIR), lambda h: (0, h)),
        out_shape=jax.ShapeDtypeStruct((HALF, KEY_VALUE_HEADS * PAIR), BF16),
        scratch_shapes=[pltpu.VMEM((HALF, ROWS), BF16)],
        compiler_params=PARAMS,
        cost_estimate=pl.CostEstimate(flops=10**8, bytes_accessed=8 * 10**5, transcendentals=0),
        name="traded_pairs",
    )(mate, landed)


def to_column(row):
    here = iota((ROWS, ROWS), 0) == iota((ROWS, ROWS), 1)
    return jnp.sum(jnp.where(here, row, 0.0), axis=1, keepdims=True)


def key_blocks(metas, rank):
    first = metas[0][0]
    count = jnp.int32(1)
    for x in (1, 2, 3):
        other = rank ^ x
        count = count + jnp.where((other < rank) & (metas[x][ROWS - 1] == first), 1, 0)
    return count


def forward_kernel(
    mate_ref, meta_own, meta_near, meta_far, meta_both, ids_own, ids_near, ids_far, ids_both,
    q_ref, landed_ref, stay_own, stay_far, stay_near, turn_own, turn_far, turn_near,
    out_ref, send_ref, merged_ref, pairs_ref,
    choose, bring, place, bias,
):
    metas = (meta_own, meta_near, meta_far, meta_both)
    rank = metas[0][ROWS + ROUNDS]

    @pl.when(pl.program_id(0) == 0)
    def _():
        mate, slot = scalars(mate_ref, 0, ROUNDS), scalars(metas[0], ROWS, ROUNDS)
        choose[...] = onehot(sent_row(mate, slot) == lanes(ROWS))
        bring[...] = onehot(landed_row(mate, slot) == lanes(ROWS))
        ids = [piece[:, :ROWS].astype(F32) for piece in (ids_own, ids_near, ids_far, ids_both)]
        column = to_column(ids[0])
        for x in range(RANKS):
            place[x] = onehot(packed_row(scalars(metas[x], ROWS, ROUNDS), 0) == lanes(ROWS))
            allowed = column == ids[x]
            if x == 0:
                allowed = allowed & (lanes(ROWS) <= position(0))
            bias[rank ^ x] = jnp.where(allowed, 0.0, MASKED)

    stay = (stay_own[...], stay_near[0], stay_far[...], stay_near[1])
    turn = (turn_own[...], turn_near[0], turn_far[...], turn_near[1])
    for x in range(RANKS):
        pairs_ref[pl.ds(pl.multiple_of((rank ^ x) * ROWS, ROWS), ROWS), :] = pick(
            place[x], jnp.concatenate([stay[x], turn[x]], axis=0)
        )
    came = landed_row(scalars(mate_ref, 0, ROUNDS), scalars(metas[0], ROWS, ROUNDS)) >= 0
    q = jnp.where(came, pick(bring[...], landed_ref[:, :WIDE]), q_ref[...])
    merged_ref[...] = q
    count = key_blocks(metas, rank)

    for n in range(1, RANKS + 1):

        @pl.when(count == n)
        def _(n=n):
            start = rank - (n - 1)
            window = pl.ds(pl.multiple_of(start * ROWS, ROWS), n * ROWS)
            k = pairs_ref[window, :HEAD_SIZE]
            v = pairs_ref[window, HEAD_SIZE:]
            mask = jnp.concatenate([bias[start + i] for i in range(n)], axis=1)
            for h in range(SHARED):
                columns = slice(h * HEAD_SIZE, (h + 1) * HEAD_SIZE)
                logits = lax.dot_general(q[:, columns], k, (((1,), (1,)), ((), ())), preferred_element_type=F32) + mask
                raised = jnp.exp2((logits - jnp.max(logits, axis=1, keepdims=True)) * EXP2_FACTOR)
                share = 1.0 / jnp.sum(raised, axis=1, keepdims=True)
                weights = (raised * share).astype(BF16)
                out_ref[:, columns] = jnp.dot(weights, v, preferred_element_type=F32).astype(BF16)

    send_ref[...] = pick(choose[...], out_ref[...])


def forward(mate, metas, q, landed, stays, turns):
    whole = lambda shape: pl.BlockSpec(shape, lambda h: (0,) * len(shape))
    pieces = [
        pl.BlockSpec((HALF, PAIR), lambda h: (0, h)),
        pl.BlockSpec((HALF, PAIR), lambda h: (0, h)),
        pl.BlockSpec((2, HALF, PAIR), lambda h: (0, 0, h)),
    ]
    return pl.pallas_call(
        forward_kernel,
        grid=(KEY_VALUE_HEADS,),
        in_specs=[SMEM] * 5 + [whole((1, META))] * 4
        + [pl.BlockSpec((ROWS, WIDE), lambda h: (0, h)), pl.BlockSpec((ROWS, BUNDLE), lambda h: (0, h))]
        + pieces
        + pieces,
        out_specs=[
            pl.BlockSpec((ROWS, WIDE), lambda h: (0, h)),
            pl.BlockSpec((ROWS, WIDE), lambda h: (0, h)),
            pl.BlockSpec((ROWS, WIDE), lambda h: (0, h)),
            pl.BlockSpec((RANKS * ROWS, PAIR), lambda h: (0, h)),
        ],
        out_shape=[
            jax.ShapeDtypeStruct((ROWS, KEY_VALUE_HEADS * WIDE), BF16),
            jax.ShapeDtypeStruct((ROWS, KEY_VALUE_HEADS * WIDE), BF16),
            jax.ShapeDtypeStruct((ROWS, KEY_VALUE_HEADS * WIDE), BF16),
            jax.ShapeDtypeStruct((RANKS * ROWS, KEY_VALUE_HEADS * PAIR), BF16),
        ],
        scratch_shapes=[
            pltpu.VMEM((ROWS, ROWS), BF16),
            pltpu.VMEM((ROWS, ROWS), BF16),
            pltpu.VMEM((RANKS, ROWS, ROWS), BF16),
            pltpu.VMEM((RANKS, ROWS, ROWS), F32),
        ],
        compiler_params=PARAMS,
        cost_estimate=pl.CostEstimate(flops=4 * 10**9, bytes_accessed=10**7, transcendentals=4 * 10**6),
        name="forward",
    )(mate, *metas, *[meta.reshape(1, META) for meta in metas], q, landed, *stays, *turns)


def backward_kernel(
    mate_ref, meta_own, meta_near, meta_far, meta_both, ids_own, ids_near, ids_far, ids_both,
    q_ref, g_ref, landed_ref, pairs_ref,
    dq_ref, send_ref, turn_keep, turn_send, stay_keep, stay_send,
    choose, bring, pack, bias, total,
):
    metas = (meta_own, meta_near, meta_far, meta_both)
    rank = metas[0][ROWS + ROUNDS]

    @pl.when(pl.program_id(0) == 0)
    def _():
        mate, slot = scalars(mate_ref, 0, ROUNDS), scalars(metas[0], ROWS, ROUNDS)
        choose[...] = onehot(sent_row(mate, slot) == lanes(ROWS))
        bring[...] = onehot(landed_row(mate, slot) == lanes(ROWS))
        ids = [piece[:, :ROWS].astype(F32) for piece in (ids_own, ids_near, ids_far, ids_both)]
        for x in range(RANKS):
            pack[x] = onehot(packed_row(scalars(metas[x], ROWS, ROUNDS), 1) == position(0))
            allowed = to_column(ids[x]) == ids[0]
            if x == 0:
                allowed = allowed & (position(0) <= lanes(ROWS))
            bias[pl.ds(pl.multiple_of((rank ^ x) * ROWS, ROWS), ROWS), :] = jnp.where(allowed, 0.0, MASKED)

    came = landed_row(scalars(mate_ref, 0, ROUNDS), scalars(metas[0], ROWS, ROUNDS)) >= 0
    g = jnp.where(came, pick(bring[...], landed_ref[...]), g_ref[...])
    count = key_blocks(metas, rank)
    total[...] = jnp.zeros_like(total)

    for n in range(1, RANKS + 1):

        @pl.when(count == n)
        def _(n=n):
            start = rank - (n - 1)
            window = pl.ds(pl.multiple_of(start * ROWS, ROWS), n * ROWS)
            k = pairs_ref[window, :HEAD_SIZE]
            v = pairs_ref[window, HEAD_SIZE:]
            mask = bias[window, :]
            inner_dims = (((1,), (1,)), ((), ()))
            lows, grads, queries, gradients = [], [], [], []
            for h in range(SHARED):
                columns = slice(h * HEAD_SIZE, (h + 1) * HEAD_SIZE)
                q_h, g_h = q_ref[:, columns], g[:, columns]
                logits = lax.dot_general(k, q_h, inner_dims, preferred_element_type=F32) + mask
                raised = jnp.exp2((logits - jnp.max(logits, axis=0, keepdims=True)) * EXP2_FACTOR)
                weights = raised * (1.0 / jnp.sum(raised, axis=0, keepdims=True))
                grad_weights = lax.dot_general(v, g_h, inner_dims, preferred_element_type=F32)
                inner = jnp.sum(weights * grad_weights, axis=0, keepdims=True)
                grad_logits = (weights * (grad_weights - inner)).astype(BF16)
                dq = lax.dot_general(grad_logits, k, (((0,), (0,)), ((), ())), preferred_element_type=F32)
                dq_ref[:, columns] = (dq * FACTOR).astype(BF16)
                lows.append(weights.astype(BF16))
                grads.append(grad_logits)
                queries.append(q_h)
                gradients.append(g_h)
            dk = jnp.dot(
                jnp.concatenate(grads, axis=1), jnp.concatenate(queries, axis=0), preferred_element_type=F32
            )
            dv = jnp.dot(
                jnp.concatenate(lows, axis=1), jnp.concatenate(gradients, axis=0), preferred_element_type=F32
            )
            total[window, :HEAD_SIZE] = (dk * FACTOR).astype(BF16)
            total[window, HEAD_SIZE:] = dv.astype(BF16)

    send_ref[:, :WIDE] = pick(choose[...], dq_ref[...])
    send_ref[:, WIDE:] = jnp.zeros((ROWS, PAIR), BF16)
    for x in range(RANKS):
        part = total[pl.ds(pl.multiple_of((rank ^ x) * ROWS, ROWS), ROWS), :]
        pieces = pick(pack[x], part)
        stay, turn = ((stay_keep, turn_keep), (stay_send, turn_send))[x & 1]
        stay[x >> 1] = pieces[:HALF]
        turn[x >> 1] = pieces[HALF:]


def backward(mate, metas, merged, g, landed, pairs):
    whole = lambda shape: pl.BlockSpec(shape, lambda h: (0,) * len(shape))
    wide = pl.BlockSpec((ROWS, WIDE), lambda h: (0, h))
    piece = pl.BlockSpec((2, HALF, PAIR), lambda h: (0, 0, h))
    piece_shape = jax.ShapeDtypeStruct((2, HALF, KEY_VALUE_HEADS * PAIR), BF16)
    return pl.pallas_call(
        backward_kernel,
        grid=(KEY_VALUE_HEADS,),
        in_specs=[SMEM] * 5 + [whole((1, META))] * 4
        + [wide, wide, wide, pl.BlockSpec((RANKS * ROWS, PAIR), lambda h: (0, h))],
        out_specs=[wide, pl.BlockSpec((ROWS, BUNDLE), lambda h: (0, h)), piece, piece, piece, piece],
        out_shape=[
            jax.ShapeDtypeStruct((ROWS, KEY_VALUE_HEADS * WIDE), BF16),
            jax.ShapeDtypeStruct((ROWS, KEY_VALUE_HEADS * BUNDLE), BF16),
            piece_shape,
            piece_shape,
            piece_shape,
            piece_shape,
        ],
        scratch_shapes=[
            pltpu.VMEM((ROWS, ROWS), BF16),
            pltpu.VMEM((ROWS, ROWS), BF16),
            pltpu.VMEM((RANKS, ROWS, ROWS), BF16),
            pltpu.VMEM((RANKS * ROWS, ROWS), F32),
            pltpu.VMEM((RANKS * ROWS, PAIR), BF16),
        ],
        compiler_params=PARAMS,
        cost_estimate=pl.CostEstimate(flops=8 * 10**9, bytes_accessed=10**7, transcendentals=4 * 10**6),
        name="backward",
    )(mate, *metas, *[meta.reshape(1, META) for meta in metas], merged, g, landed, pairs)


def returning_kernel(mate_ref, send_ref, own_ref, near_ref, far_ref, out_ref):
    total = own_ref[0].astype(F32) + near_ref[0].astype(F32) + far_ref[...].astype(F32)
    choose = onehot(sent_turn(scalars(mate_ref, 0, ROUNDS)) == lanes(HALF))
    out_ref[...] = pick(choose, total.astype(BF16))


def returning(mate, send, own, near, far):
    first = pl.BlockSpec((1, HALF, PAIR), lambda h: (0, 0, h))
    return pl.pallas_call(
        returning_kernel,
        grid=(KEY_VALUE_HEADS,),
        in_specs=[SMEM, pl.BlockSpec(memory_space=pl.ANY), first, first, pl.BlockSpec((HALF, PAIR), lambda h: (0, h))],
        out_specs=pl.BlockSpec((ROWS, PAIR), lambda h: (0, 3 * h + 2)),
        out_shape=jax.ShapeDtypeStruct(send.shape, BF16),
        input_output_aliases={1: 0},
        compiler_params=PARAMS,
        cost_estimate=pl.CostEstimate(flops=10**8, bytes_accessed=10**6, transcendentals=0),
        name="returning",
    )(mate, send, own, near, far)


def merge_kernel(mate_ref, slot_ref, own_ref, landed_ref, out_ref, bring):
    row = landed_row(scalars(mate_ref, 0, ROUNDS), scalars(slot_ref, 0, ROUNDS))

    @pl.when(pl.program_id(0) == 0)
    def _():
        bring[...] = onehot(row == lanes(ROWS))

    out_ref[...] = jnp.where(row >= 0, pick(bring[...], landed_ref[...]), own_ref[...])


def merge(mate, slot, own, landed):
    wide = pl.BlockSpec((ROWS, WIDE), lambda h: (0, h))
    return pl.pallas_call(
        merge_kernel,
        grid=(KEY_VALUE_HEADS,),
        in_specs=[SMEM, SMEM, wide, wide],
        out_specs=wide,
        out_shape=jax.ShapeDtypeStruct(own.shape, BF16),
        scratch_shapes=[pltpu.VMEM((ROWS, ROWS), BF16)],
        compiler_params=PARAMS,
        cost_estimate=pl.CostEstimate(flops=5 * 10**8, bytes_accessed=3 * 10**6, transcendentals=0),
        name="merge",
    )(mate, slot, own, landed)


def finish_kernel(
    mate_ref, slot_ref, dq_ref, landed_ref, own_ref, near_ref, far_ref, grad_q, grad_k, grad_v, bring, place
):
    row = landed_row(scalars(mate_ref, 0, ROUNDS), scalars(slot_ref, 0, ROUNDS))

    @pl.when(pl.program_id(0) == 0)
    def _():
        bring[...] = onehot(row == lanes(ROWS))
        place[...] = onehot(packed_row(scalars(slot_ref, 0, ROUNDS), 0) == lanes(HALF))

    total = own_ref[0].astype(F32) + near_ref[0].astype(F32) + far_ref[...].astype(F32)
    came = pick(bring[...], landed_ref[...])
    grad_q[...] = jnp.where(row >= 0, came[:, :WIDE], dq_ref[...])
    pairs = jnp.where(row >= 0, came[:, WIDE:], pick(place[...], total.astype(BF16)))
    grad_k[...] = pairs[:, :HEAD_SIZE]
    grad_v[...] = pairs[:, HEAD_SIZE:]


def finish(mate, slot, dq, landed, own, near, far):
    wide = pl.BlockSpec((ROWS, WIDE), lambda h: (0, h))
    head = pl.BlockSpec((ROWS, HEAD_SIZE), lambda h: (0, h))
    first = pl.BlockSpec((1, HALF, PAIR), lambda h: (0, 0, h))
    narrow = jax.ShapeDtypeStruct((ROWS, KEY_VALUE_HEADS * HEAD_SIZE), BF16)
    return pl.pallas_call(
        finish_kernel,
        grid=(KEY_VALUE_HEADS,),
        in_specs=[
            SMEM, SMEM, wide, pl.BlockSpec((ROWS, BUNDLE), lambda h: (0, h)),
            first, first, pl.BlockSpec((HALF, PAIR), lambda h: (0, h)),
        ],
        out_specs=[wide, head, head],
        out_shape=[jax.ShapeDtypeStruct(dq.shape, BF16), narrow, narrow],
        scratch_shapes=[pltpu.VMEM((ROWS, ROWS), BF16), pltpu.VMEM((ROWS, HALF), BF16)],
        compiler_params=PARAMS,
        cost_estimate=pl.CostEstimate(flops=8 * 10**8, bytes_accessed=5 * 10**6, transcendentals=0),
        name="finish",
    )(mate, slot, dq, landed, own, near, far)


def exchange(rows):
    blocks = rows.reshape(GROUPS, BLOCK, rows.shape[-1])
    return lax.all_to_all(blocks, "dp", split_axis=0, concat_axis=0, tiled=True).reshape(rows.shape)


def across(array):
    return lax.ppermute(array, "sp", [(i, i ^ 2) for i in range(RANKS)])


def beside(array):
    return lax.ppermute(array, "sp", [(i, i ^ 1) for i in range(RANKS)])


def spread(array):
    far = across(array)
    near = beside(jnp.stack([array, far]))
    return array, far, near


def collect(keep, send):
    near = beside(send)
    partial = (keep[1].astype(F32) + near[1].astype(F32)).astype(BF16)
    return keep, near, across(partial)


def body(queries, keys, values, cotangent, doc_ids, partners, swap_slots):
    q, k, v, g = queries[0], keys[0], values[0], cotangent[0]
    mate = partners.reshape(ROUNDS)
    slot = swap_slots.reshape(ROUNDS)
    rank = lax.axis_index("sp").astype(jnp.int32).reshape(1)
    meta = jnp.concatenate(
        [doc_ids.reshape(ROWS), slot, rank, jnp.zeros((META - ROWS - ROUNDS - 1,), jnp.int32)]
    )

    first, second, stay = outgoing(mate, slot, q, k, v, g)
    landed = exchange(first)
    meta_own, meta_far, meta_near = spread(meta)
    metas = (meta_own, meta_near[0], meta_far, meta_near[1])
    stays = spread(stay)
    landed, second = lax.optimization_barrier((landed, second))
    landed_g = exchange(second)
    turns = spread(traded_pairs(mate, landed))
    out, send, merged, pairs = forward(mate, metas, q, landed, stays, turns)
    landed_g, send = lax.optimization_barrier((landed_g, send))
    landed_out = exchange(send)
    dq, send, turn_keep, turn_send, stay_keep, stay_send = backward(mate, metas, merged, g, landed_g, pairs)
    send = returning(mate, send, *collect(turn_keep, turn_send))
    landed_out, send = lax.optimization_barrier((landed_out, send))
    landed = exchange(send)
    attended = merge(mate, slot, out, landed_out)
    grad_q, grad_k, grad_v = finish(mate, slot, dq, landed, *collect(stay_keep, stay_send))
    return attended[None], grad_q[None], grad_k[None], grad_v[None]


def solution(mesh):
    rows = P("dp", "sp", None)
    return jax.shard_map(
        body,
        mesh=mesh,
        in_specs=(rows, rows, rows, rows, P("dp", "sp"), P(None, "dp"), rows),
        out_specs=(rows, rows, rows, rows),
        check_vma=False,
    )
```

```python
import jax
import jax.numpy as jnp
from jax import lax
from jax.experimental import pallas as pl
from jax.experimental.pallas import tpu as pltpu
from jax.sharding import PartitionSpec as P

KEY_VALUE_HEADS = 4
SHARED = 4
HEAD_SIZE = 128
BLOCK = 8
ROUNDS = 16
ROWS = 256
HALF = ROUNDS * BLOCK
GROUPS = 32
RANKS = 4
WIDE = SHARED * HEAD_SIZE
PAIR = 2 * HEAD_SIZE
BUNDLE = WIDE + PAIR
CARGO = 2 * WIDE + PAIR
META = 384
KEYS = 128
EARLIER = (RANKS - 1) * ROWS // KEYS
FACTOR = HEAD_SIZE ** (-0.5)
EXP2_FACTOR = FACTOR * 1.4426950408889634
MASKED = -1e30
BF16 = jnp.bfloat16
F32 = jnp.float32

SMEM = pl.BlockSpec(memory_space=pltpu.SMEM)
VMEM = pl.BlockSpec(memory_space=pltpu.VMEM)
HBM = pl.BlockSpec(memory_space=pl.ANY)
PARAMS = pltpu.CompilerParams(vmem_limit_bytes=24 * 1024 * 1024)


def in_hbm(array):
    return pltpu.with_memory_space_constraint(array, pltpu.HBM)


def in_vmem(array):
    return pltpu.with_memory_space_constraint(array, pltpu.VMEM)


def iota(shape, axis):
    return lax.broadcasted_iota(jnp.int32, shape, axis)


def onehot(hit):
    return jnp.where(hit, 1.0, 0.0).astype(BF16)


def pick(matrix, rows):
    return jnp.dot(matrix, rows, preferred_element_type=F32).astype(BF16)


def part(h, first, width, whole):
    return pl.ds(pl.multiple_of(h * whole + first, HEAD_SIZE), width)


def lanes(width):
    return iota((1, width), 1)


def matching(value, keys, results):
    found = jnp.full_like(value, -1)
    for key, result in zip(keys, results):
        found = jnp.where(value == key, result, found)
    return found


def rows_at(block, place):
    return jnp.where(block >= 0, block * BLOCK + (place & 7), -1)


def placing(target, count):
    return onehot(target == iota((count, target.shape[1]), 0))


def choose_sent(mate, slot):
    place = lanes(ROWS)
    return placing(rows_at(matching(place >> 3, slot, mate), place), ROWS)


def choose_landed(mate, slot):
    place = lanes(ROWS)
    return placing(rows_at(matching(place >> 3, mate, slot), place), ROWS)


def choose_turns(mate):
    place = lanes(ROWS)
    return placing(rows_at(matching(place >> 3, mate, range(ROUNDS)), place), HALF)


def choose_sent_turns(mate):
    place = lanes(HALF)
    return placing(rows_at(matching(place >> 3, range(ROUNDS), mate), place), ROWS)


def packed_row(slot):
    place = lanes(ROWS)
    block = place >> 3
    turn = matching(block, slot, range(ROUNDS))
    lower = jnp.zeros_like(place)
    for t in range(ROUNDS):
        lower = lower + jnp.where(block > slot[t], 1, 0)
    return jnp.where(turn >= 0, HALF + turn * BLOCK, (block - lower) * BLOCK) + (place & 7)


def packing(slot, count=ROWS):
    return placing(packed_row(slot), count)


def unpacking(slot):
    hit = jnp.where(packed_row(slot) == iota((ROWS, ROWS), 0), 1.0, 0.0)
    return hit.T.astype(BF16)


def share_landed(matrix):
    return jnp.broadcast_to(jnp.sum(matrix.astype(F32), axis=1, keepdims=True), (ROWS, HEAD_SIZE))


def replaced(came, landed, own):
    mask = jnp.concatenate([came] * (own.shape[1] // HEAD_SIZE), axis=1)
    return jnp.where(mask > 0.5, landed, own.astype(F32)).astype(BF16)


def scalars(ref, first, count):
    return [ref[first + t] for t in range(count)]


def outgoing_kernel(mate_ref, slot_ref, q_ref, k_ref, v_ref, g_ref, send_ref, stay_ref, choose, keep):
    @pl.when(pl.program_id(0) == 0)
    def _():
        mate, slot = scalars(mate_ref, 0, ROUNDS), scalars(slot_ref, 0, ROUNDS)
        choose[...] = choose_sent(mate, slot)
        keep[...] = packing(slot, HALF)

    pairs = jnp.concatenate([k_ref[...], v_ref[...]], axis=1)
    send_ref[...] = pick(choose[...], jnp.concatenate([q_ref[...], pairs, g_ref[...]], axis=1))
    stay_ref[...] = pick(keep[...], pairs)


def outgoing(mate, slot, q, k, v, g):
    return pl.pallas_call(
        outgoing_kernel,
        grid=(KEY_VALUE_HEADS,),
        in_specs=[
            SMEM,
            SMEM,
            pl.BlockSpec((ROWS, WIDE), lambda h: (0, h)),
            pl.BlockSpec((ROWS, HEAD_SIZE), lambda h: (0, h)),
            pl.BlockSpec((ROWS, HEAD_SIZE), lambda h: (0, h)),
            pl.BlockSpec((ROWS, WIDE), lambda h: (0, h)),
        ],
        out_specs=[
            pl.BlockSpec((ROWS, CARGO), lambda h: (0, h)),
            pl.BlockSpec((HALF, PAIR), lambda h: (0, h)),
        ],
        out_shape=[
            pltpu.HBM((ROWS, KEY_VALUE_HEADS * CARGO), BF16),
            pltpu.VMEM((HALF, KEY_VALUE_HEADS * PAIR), BF16),
        ],
        scratch_shapes=[pltpu.VMEM((ROWS, ROWS), BF16), pltpu.VMEM((HALF, ROWS), BF16)],
        compiler_params=PARAMS,
        cost_estimate=pl.CostEstimate(flops=10**9, bytes_accessed=5 * 10**6, transcendentals=0),
        name="outgoing",
    )(mate, slot, in_hbm(q), in_hbm(k), in_hbm(v), in_hbm(g))


def traded_pairs_kernel(mate_ref, landed_ref, out_ref):
    choose = choose_turns(scalars(mate_ref, 0, ROUNDS))
    for h in range(KEY_VALUE_HEADS):
        out_ref[:, part(h, 0, PAIR, PAIR)] = pick(choose, landed_ref[:, part(h, WIDE, PAIR, CARGO)])


def traded_pairs(mate, landed):
    return pl.pallas_call(
        traded_pairs_kernel,
        in_specs=[SMEM, VMEM],
        out_specs=VMEM,
        out_shape=pltpu.VMEM((HALF, KEY_VALUE_HEADS * PAIR), BF16),
        compiler_params=PARAMS,
        cost_estimate=pl.CostEstimate(flops=10**8, bytes_accessed=8 * 10**5, transcendentals=0),
        name="traded_pairs",
    )(mate, in_vmem(landed))


def to_column(row):
    here = iota((ROWS, ROWS), 0) == iota((ROWS, ROWS), 1)
    return jnp.sum(jnp.where(here, row, 0.0), axis=1, keepdims=True)


def earlier_blocks(metas, rank):
    first = metas[0][0]
    count = jnp.int32(0)
    for x in (1, 2, 3):
        for last in range(KEYS - 1, ROWS, KEYS):
            count = count + jnp.where(((rank ^ x) < rank) & (metas[x][last] == first), 1, 0)
    return count


def fill_mask(mask, metas_ids, rank):
    ids = [piece[:, :ROWS].astype(F32) for piece in metas_ids]
    for x in range(RANKS):
        allowed = to_column(ids[x]) == ids[0]
        if x == 0:
            allowed = allowed & (iota((ROWS, 1), 0) <= lanes(ROWS))
        mask[pl.ds(pl.multiple_of((rank ^ x) * ROWS, ROWS), ROWS), :] = jnp.where(allowed, 0.0, MASKED)


INNER = (((1,), (1,)), ((), ()))


def forward_kernel(
    mate_ref, meta_own, meta_near, meta_far, meta_both, ids_own, ids_near, ids_far, ids_both,
    q_hbm, g_hbm, landed_ref, stay_own, stay_near, stay_far, stay_both, turn_own, turn_near, turn_far, turn_both,
    out_hbm, send_hbm, q_kept, g_kept, pairs_kept, stats_hbm,
    out_ref, send_ref, q_ref, g_ref, pairs_ref, stats_ref, bring, place, mask, came, q_arrived, g_arrived, left,
):
    q_copy = pltpu.make_async_copy(q_hbm, q_ref, q_arrived)
    g_copy = pltpu.make_async_copy(g_hbm, g_ref, g_arrived)
    q_copy.start()
    g_copy.start()
    metas = (meta_own, meta_near, meta_far, meta_both)
    rank = metas[0][ROWS + ROUNDS]
    count = earlier_blocks(metas, rank)
    mate, slot = scalars(mate_ref, 0, ROUNDS), scalars(metas[0], ROWS, ROUNDS)
    choose = choose_sent(mate, slot)
    bring[...] = choose_landed(mate, slot)
    came[...] = share_landed(bring[...])
    fill_mask(mask, (ids_own, ids_near, ids_far, ids_both), rank)
    stay = (stay_own, stay_near, stay_far, stay_both)
    turn = (turn_own, turn_near, turn_far, turn_both)
    for x in range(RANKS):
        other = rank ^ x

        @pl.when((other <= rank) & ((rank - other - 1) * ROWS < count * KEYS))
        def _(x=x, other=other):
            rows = jnp.concatenate([stay[x][...], turn[x][...]], axis=0)
            place[...] = unpacking(scalars(metas[x], ROWS, ROUNDS))
            pairs_ref[pl.ds(pl.multiple_of(other * ROWS, ROWS), ROWS), :] = pick(place[...], rows)

    q_copy.wait()
    g_copy.wait()

    def leave(h, turn, source, target, whole):
        columns = part(h, 0, whole, whole)
        return pltpu.make_async_copy(source.at[:, columns], target.at[:, columns], left.at[turn, h])

    def leave_early(h):
        return [leave(h, 0, q_ref, q_kept, WIDE), leave(h, 1, g_ref, g_kept, WIDE), leave(h, 2, pairs_ref, pairs_kept, PAIR)]

    def leave_late(h):
        return [leave(h, 3, out_ref, out_hbm, WIDE), leave(h, 4, send_ref, send_hbm, WIDE)]

    def head(h, carry):
        wide = part(h, 0, WIDE, WIDE)
        came_q = jnp.dot(bring[...], landed_ref[:, part(h, 0, WIDE, CARGO)], preferred_element_type=F32)
        came_g = jnp.dot(bring[...], landed_ref[:, part(h, BUNDLE, WIDE, CARGO)], preferred_element_type=F32)
        q_ref[:, wide] = replaced(came[...], came_q, q_ref[:, wide])
        g_ref[:, wide] = replaced(came[...], came_g, g_ref[:, wide])
        for copy in leave_early(h):
            copy.start()

        for n in range(EARLIER + 1):

            @pl.when(count == n)
            def _(n=n):
                window = pl.ds(pl.multiple_of(rank * ROWS - n * KEYS, KEYS), n * KEYS + ROWS)
                k = pairs_ref[window, part(h, 0, HEAD_SIZE, PAIR)]
                v_turned = pairs_ref[window, part(h, HEAD_SIZE, HEAD_SIZE, PAIR)].T
                shifts, inners = [], []
                for i in range(SHARED):
                    columns = part(h, i * HEAD_SIZE, HEAD_SIZE, WIDE)
                    logits = lax.dot_general(k, q_ref[:, columns], INNER, preferred_element_type=F32) + mask[window, :]
                    top = jnp.max(logits, axis=0, keepdims=True)
                    raised = jnp.exp2((logits - top) * EXP2_FACTOR)
                    total = jnp.sum(raised, axis=0, keepdims=True)
                    out = jnp.dot(v_turned, raised.astype(BF16), preferred_element_type=F32) * (1.0 / total)
                    inners.append(jnp.sum(out * g_ref[:, columns].T.astype(F32), axis=0, keepdims=True))
                    shifts.append(top * EXP2_FACTOR + jnp.log2(total))
                    out_ref[:, columns] = out.astype(BF16).T
                stats_ref[pl.ds(pl.multiple_of(h * 2 * SHARED, 2 * SHARED), 2 * SHARED), :] = jnp.concatenate(
                    shifts + inners, axis=0
                )

        send_ref[:, wide] = pick(choose, out_ref[:, wide])
        for copy in leave_late(h):
            copy.start()
        return carry

    lax.fori_loop(0, KEY_VALUE_HEADS, head, 0)
    stats_copy = pltpu.make_async_copy(stats_ref, stats_hbm, q_arrived)
    stats_copy.start()
    for h in range(KEY_VALUE_HEADS):
        for copy in leave_early(h) + leave_late(h):
            copy.wait()
    stats_copy.wait()


def forward(mate, metas, q, g, landed, stays, turns):
    wide = (ROWS, KEY_VALUE_HEADS * WIDE)
    return pl.pallas_call(
        forward_kernel,
        in_specs=[SMEM] * 5 + [VMEM] * 4 + [HBM] * 2 + [VMEM] * (1 + 2 * RANKS),
        out_specs=[HBM] * 6,
        out_shape=[
            pltpu.HBM(wide, BF16),
            pltpu.HBM(wide, BF16),
            pltpu.HBM(wide, BF16),
            pltpu.HBM(wide, BF16),
            pltpu.HBM((RANKS * ROWS, KEY_VALUE_HEADS * PAIR), BF16),
            pltpu.HBM((KEY_VALUE_HEADS * 2 * SHARED, ROWS), F32),
        ],
        scratch_shapes=[
            pltpu.VMEM(wide, BF16),
            pltpu.VMEM(wide, BF16),
            pltpu.VMEM(wide, BF16),
            pltpu.VMEM(wide, BF16),
            pltpu.VMEM((RANKS * ROWS, KEY_VALUE_HEADS * PAIR), BF16),
            pltpu.VMEM((KEY_VALUE_HEADS * 2 * SHARED, ROWS), F32),
            pltpu.VMEM((ROWS, ROWS), BF16),
            pltpu.VMEM((ROWS, ROWS), BF16),
            pltpu.VMEM((RANKS * ROWS, ROWS), F32),
            pltpu.VMEM((ROWS, HEAD_SIZE), F32),
            pltpu.SemaphoreType.DMA,
            pltpu.SemaphoreType.DMA,
            pltpu.SemaphoreType.DMA((5, KEY_VALUE_HEADS)),
        ],
        compiler_params=PARAMS,
        cost_estimate=pl.CostEstimate(flops=4 * 10**9, bytes_accessed=10**7, transcendentals=4 * 10**6),
        name="forward",
    )(
        mate, *metas, *[in_vmem(meta.reshape(1, META)) for meta in metas],
        in_hbm(q), in_hbm(g), in_vmem(landed), *[in_vmem(x) for x in (*stays, *turns)],
    )


def backward_kernel(
    mate_ref, meta_own, meta_near, meta_far, meta_both, ids_own, ids_near, ids_far, ids_both,
    q_hbm, g_hbm, pairs_hbm, stats_hbm,
    dq_hbm, send_ref, turn_keep, turn_send, keep_hbm, send_hbm,
    q_ref, g_ref, pairs_ref, stats_ref, dq_ref, stay_keep, stay_send, mask, total, arrived, stats_arrived, left, stay_left,
):
    def arrive(h, turn, source, target, whole):
        columns = part(h, 0, whole, whole)
        return pltpu.make_async_copy(source.at[:, columns], target.at[:, columns], arrived.at[turn, h])

    def arrivals(h):
        return [arrive(h, 0, pairs_hbm, pairs_ref, PAIR), arrive(h, 1, q_hbm, q_ref, WIDE), arrive(h, 2, g_hbm, g_ref, WIDE)]

    stats_copy = pltpu.make_async_copy(stats_hbm, stats_ref, stats_arrived)
    stats_copy.start()
    for h in range(KEY_VALUE_HEADS):
        for copy in arrivals(h):
            copy.start()
    metas = (meta_own, meta_near, meta_far, meta_both)
    rank = metas[0][ROWS + ROUNDS]
    count = earlier_blocks(metas, rank)
    choose = choose_sent(scalars(mate_ref, 0, ROUNDS), scalars(metas[0], ROWS, ROUNDS))
    fill_mask(mask, (ids_own, ids_near, ids_far, ids_both), rank)
    total[...] = jnp.zeros_like(total)

    def leave(h):
        columns = part(h, 0, WIDE, WIDE)
        return pltpu.make_async_copy(dq_ref.at[:, columns], dq_hbm.at[:, columns], left.at[h])

    stats_copy.wait()

    def head(h, carry):
        for copy in arrivals(h):
            copy.wait()

        for n in range(EARLIER + 1):

            @pl.when(count == n)
            def _(n=n):
                window = pl.ds(pl.multiple_of(rank * ROWS - n * KEYS, KEYS), n * KEYS + ROWS)
                k_columns = part(h, 0, HEAD_SIZE, PAIR)
                v_columns = part(h, HEAD_SIZE, HEAD_SIZE, PAIR)
                k = pairs_ref[window, k_columns]
                v = pairs_ref[window, v_columns]
                k_turned = k.T
                stats = stats_ref[pl.ds(pl.multiple_of(h * 2 * SHARED, 2 * SHARED), 2 * SHARED), :]
                lows, grads, queries, gradients = [], [], [], []
                for i in range(SHARED):
                    columns = part(h, i * HEAD_SIZE, HEAD_SIZE, WIDE)
                    q, g = q_ref[:, columns], g_ref[:, columns]
                    logits = lax.dot_general(k, q, INNER, preferred_element_type=F32)
                    weights = jnp.exp2(logits * EXP2_FACTOR - stats[i : i + 1, :] + mask[window, :])
                    grad_weights = lax.dot_general(v, g, INNER, preferred_element_type=F32)
                    inner = stats[SHARED + i : SHARED + i + 1, :]
                    grad_logits = (weights * (grad_weights - inner)).astype(BF16)
                    dq = jnp.dot(k_turned, grad_logits, preferred_element_type=F32) * FACTOR
                    dq_ref[:, columns] = dq.astype(BF16).T
                    lows.append(weights.astype(BF16))
                    grads.append(grad_logits)
                    queries.append(q)
                    gradients.append(g)
                dk = jnp.dot(
                    jnp.concatenate(grads, axis=1), jnp.concatenate(queries, axis=0), preferred_element_type=F32
                )
                dv = jnp.dot(
                    jnp.concatenate(lows, axis=1), jnp.concatenate(gradients, axis=0), preferred_element_type=F32
                )
                total[window, k_columns] = (dk * FACTOR).astype(BF16)
                total[window, v_columns] = dv.astype(BF16)

        leave(h).start()
        wide = part(h, 0, WIDE, WIDE)
        send_ref[:, wide] = pick(choose, dq_ref[:, wide])
        return carry

    lax.fori_loop(0, KEY_VALUE_HEADS, head, 0)
    for x in range(RANKS):
        rows = total[pl.ds(pl.multiple_of((rank ^ x) * ROWS, ROWS), ROWS), :]
        pieces = pick(packing(scalars(metas[x], ROWS, ROUNDS)), rows)
        stay, turn = ((stay_keep, turn_keep), (stay_send, turn_send))[x & 1]
        stay[x >> 1] = pieces[:HALF]
        turn[x >> 1] = pieces[HALF:]
    leaving = [
        pltpu.make_async_copy(stay_keep, keep_hbm, stay_left.at[0]),
        pltpu.make_async_copy(stay_send, send_hbm, stay_left.at[1]),
    ]
    for copy in leaving:
        copy.start()
    for copy in leaving + [leave(h) for h in range(KEY_VALUE_HEADS)]:
        copy.wait()


def backward(mate, metas, q, g, pairs, stats):
    wide = (ROWS, KEY_VALUE_HEADS * WIDE)
    piece = (2, HALF, KEY_VALUE_HEADS * PAIR)
    return pl.pallas_call(
        backward_kernel,
        in_specs=[SMEM] * 5 + [VMEM] * 4 + [HBM] * 4,
        out_specs=[HBM, VMEM, VMEM, VMEM, HBM, HBM],
        out_shape=[
            pltpu.HBM(wide, BF16),
            pltpu.VMEM(wide, BF16),
            pltpu.VMEM(piece, BF16),
            pltpu.VMEM(piece, BF16),
            pltpu.HBM(piece, BF16),
            pltpu.HBM(piece, BF16),
        ],
        scratch_shapes=[
            pltpu.VMEM(wide, BF16),
            pltpu.VMEM(wide, BF16),
            pltpu.VMEM(pairs.shape, BF16),
            pltpu.VMEM(stats.shape, F32),
            pltpu.VMEM(wide, BF16),
            pltpu.VMEM(piece, BF16),
            pltpu.VMEM(piece, BF16),
            pltpu.VMEM((RANKS * ROWS, ROWS), F32),
            pltpu.VMEM(pairs.shape, BF16),
            pltpu.SemaphoreType.DMA((3, KEY_VALUE_HEADS)),
            pltpu.SemaphoreType.DMA,
            pltpu.SemaphoreType.DMA((KEY_VALUE_HEADS,)),
            pltpu.SemaphoreType.DMA((2,)),
        ],
        compiler_params=PARAMS,
        cost_estimate=pl.CostEstimate(flops=8 * 10**9, bytes_accessed=10**7, transcendentals=4 * 10**6),
        name="backward",
    )(
        mate, *metas, *[in_vmem(meta.reshape(1, META)) for meta in metas],
        in_hbm(q), in_hbm(g), in_hbm(pairs), in_hbm(stats),
    )


def returning_kernel(mate_ref, dq_ref, own_ref, near_ref, far_ref, send_ref):
    choose = choose_sent_turns(scalars(mate_ref, 0, ROUNDS))
    for h in range(KEY_VALUE_HEADS):
        columns = part(h, 0, PAIR, PAIR)
        total = (
            own_ref[0, :, columns].astype(F32) + near_ref[0, :, columns].astype(F32) + far_ref[:, columns].astype(F32)
        )
        send_ref[:, part(h, 0, WIDE, BUNDLE)] = dq_ref[:, part(h, 0, WIDE, WIDE)]
        send_ref[:, part(h, WIDE, PAIR, BUNDLE)] = pick(choose, total.astype(BF16))


def returning(mate, dq, own, near, far):
    return pl.pallas_call(
        returning_kernel,
        in_specs=[SMEM] + [VMEM] * 4,
        out_specs=VMEM,
        out_shape=pltpu.VMEM((ROWS, KEY_VALUE_HEADS * BUNDLE), BF16),
        compiler_params=PARAMS,
        cost_estimate=pl.CostEstimate(flops=10**8, bytes_accessed=10**6, transcendentals=0),
        name="returning",
    )(mate, in_vmem(dq), in_vmem(own), in_vmem(near), in_vmem(far))


def merge_kernel(mate_ref, slot_ref, own_ref, landed_ref, out_ref, bring, came):
    @pl.when(pl.program_id(0) == 0)
    def _():
        bring[...] = choose_landed(scalars(mate_ref, 0, ROUNDS), scalars(slot_ref, 0, ROUNDS))
        came[...] = share_landed(bring[...])

    landed = jnp.dot(bring[...], landed_ref[...], preferred_element_type=F32)
    out_ref[...] = replaced(came[...], landed, own_ref[...])


def merge(mate, slot, own, landed):
    wide = pl.BlockSpec((ROWS, WIDE), lambda h: (0, h))
    return pl.pallas_call(
        merge_kernel,
        grid=(KEY_VALUE_HEADS,),
        in_specs=[SMEM, SMEM, wide, wide],
        out_specs=wide,
        out_shape=pltpu.HBM(own.shape, BF16),
        scratch_shapes=[pltpu.VMEM((ROWS, ROWS), BF16), pltpu.VMEM((ROWS, HEAD_SIZE), F32)],
        compiler_params=PARAMS,
        cost_estimate=pl.CostEstimate(flops=5 * 10**8, bytes_accessed=3 * 10**6, transcendentals=0),
        name="merge",
    )(mate, slot, in_hbm(own), in_vmem(landed))


def finish_kernel(
    mate_ref, slot_ref, dq_hbm, landed_ref, own_hbm, near_ref, far_ref,
    grad_q, grad_k, grad_v,
    dq_ref, own_ref, k_ref, v_ref, arrived, left,
):
    own_arriving = pltpu.make_async_copy(own_hbm, own_ref, arrived.at[1])
    own_arriving.start()
    arriving = pltpu.make_async_copy(dq_hbm, dq_ref, arrived.at[0])
    arriving.start()
    mate, slot = scalars(mate_ref, 0, ROUNDS), scalars(slot_ref, 0, ROUNDS)
    bring = choose_landed(mate, slot)
    came = share_landed(bring)
    place = unpacking(slot)[:, :HALF]
    own_arriving.wait()
    for h in range(KEY_VALUE_HEADS):
        columns = part(h, 0, PAIR, PAIR)
        total = (
            own_ref[0, :, columns].astype(F32) + near_ref[0, :, columns].astype(F32) + far_ref[:, columns].astype(F32)
        )
        landed = jnp.dot(bring, landed_ref[:, part(h, WIDE, PAIR, BUNDLE)], preferred_element_type=F32)
        pairs = (jnp.dot(place, total.astype(BF16), preferred_element_type=F32) + landed).astype(BF16)
        k_ref[:, part(h, 0, HEAD_SIZE, HEAD_SIZE)] = pairs[:, :HEAD_SIZE]
        v_ref[:, part(h, 0, HEAD_SIZE, HEAD_SIZE)] = pairs[:, HEAD_SIZE:]
    leaving = [
        pltpu.make_async_copy(k_ref, grad_k, left.at[0]),
        pltpu.make_async_copy(v_ref, grad_v, left.at[1]),
    ]
    for copy in leaving:
        copy.start()
    arriving.wait()
    for h in range(KEY_VALUE_HEADS):
        columns = part(h, 0, WIDE, WIDE)
        landed = jnp.dot(bring, landed_ref[:, part(h, 0, WIDE, BUNDLE)], preferred_element_type=F32)
        dq_ref[:, columns] = replaced(came, landed, dq_ref[:, columns])
        copy = pltpu.make_async_copy(dq_ref.at[:, columns], grad_q.at[:, columns], left.at[2 + h])
        copy.start()
        leaving.append(copy)
    for copy in leaving:
        copy.wait()


def finish(mate, slot, dq, landed, own, near, far):
    narrow = (ROWS, KEY_VALUE_HEADS * HEAD_SIZE)
    return pl.pallas_call(
        finish_kernel,
        in_specs=[SMEM, SMEM, HBM, VMEM, HBM, VMEM, VMEM],
        out_specs=[HBM] * 3,
        out_shape=[pltpu.HBM(dq.shape, BF16), pltpu.HBM(narrow, BF16), pltpu.HBM(narrow, BF16)],
        scratch_shapes=[
            pltpu.VMEM(dq.shape, BF16),
            pltpu.VMEM(own.shape, BF16),
            pltpu.VMEM(narrow, BF16),
            pltpu.VMEM(narrow, BF16),
            pltpu.SemaphoreType.DMA((2,)),
            pltpu.SemaphoreType.DMA((2 + KEY_VALUE_HEADS,)),
        ],
        compiler_params=PARAMS,
        cost_estimate=pl.CostEstimate(flops=8 * 10**8, bytes_accessed=5 * 10**6, transcendentals=0),
        name="finish",
    )(mate, slot, in_hbm(dq), in_vmem(landed), in_hbm(own), in_vmem(near), in_vmem(far))


def exchange(rows):
    blocks = rows.reshape(GROUPS, BLOCK, rows.shape[-1])
    return lax.all_to_all(blocks, "dp", split_axis=0, concat_axis=0, tiled=True).reshape(rows.shape)


def across(array):
    return lax.ppermute(array, "sp", [(i, i ^ 2) for i in range(RANKS)])


def beside(array):
    return lax.ppermute(array, "sp", [(i, i ^ 1) for i in range(RANKS)])


def spread(array):
    far = across(array)
    return array, beside(array), far, beside(far)


def collect(keep, send):
    near = beside(send)
    partial = (keep[1].astype(F32) + near[1].astype(F32)).astype(BF16)
    return keep, near, across(partial)


def body(queries, keys, values, cotangent, doc_ids, partners, swap_slots):
    q, k, v, g = queries[0], keys[0], values[0], cotangent[0]
    mate = in_hbm(partners.reshape(ROUNDS))
    slots = swap_slots.reshape(ROUNDS)
    slot = in_hbm(slots)
    rank = lax.axis_index("sp").astype(jnp.int32).reshape(1)
    meta = jnp.concatenate(
        [doc_ids.reshape(ROWS), slots, rank, jnp.zeros((META - ROWS - ROUNDS - 1,), jnp.int32)]
    )

    metas = meta, beside(meta), across(meta), lax.ppermute(meta, "sp", [(i, i ^ 3) for i in range(RANKS)])
    send, stay = outgoing(mate, slot, q, k, v, g)
    send, metas = lax.optimization_barrier((send, metas))
    landed = exchange(send)
    stays = spread(stay)
    landed, stays = lax.optimization_barrier((landed, stays))
    turns = spread(traded_pairs(mate, landed))
    out, send, *kept = forward(mate, metas, q, g, landed, stays, turns)
    landed_out = exchange(send)
    dq, send, turn_keep, turn_send, stay_keep, stay_send = backward(mate, metas, *kept)
    landed_out, turn_send = lax.optimization_barrier((landed_out, turn_send))
    send = returning(mate, send, *collect(turn_keep, turn_send))
    landed = exchange(send)
    attended = merge(mate, slot, out, landed_out)
    grad_q, grad_k, grad_v = finish(mate, slot, dq, landed, *collect(stay_keep, stay_send))
    return attended[None], grad_q[None], grad_k[None], grad_v[None]


def solution(mesh):
    rows = P("dp", "sp", None)
    return jax.shard_map(
        body,
        mesh=mesh,
        in_specs=(rows, rows, rows, rows, P("dp", "sp"), P(None, "dp"), rows),
        out_specs=(rows, rows, rows, rows),
        check_vma=False,
    )
```

```python
import jax
import jax.numpy as jnp
from jax import lax
from jax.experimental import pallas as pl
from jax.experimental.pallas import tpu as pltpu
from jax.sharding import PartitionSpec as P

KEY_VALUE_HEADS = 4
SHARED = 4
HEAD_SIZE = 128
BLOCK = 8
ROUNDS = 16
ROWS = 256
HALF = ROUNDS * BLOCK
GROUPS = 32
RANKS = 4
WIDE = SHARED * HEAD_SIZE
PAIR = 2 * HEAD_SIZE
BUNDLE = WIDE + PAIR
CARGO = 2 * WIDE + PAIR
META = 384
KEYS = 128
EARLIER = (RANKS - 1) * ROWS // KEYS
FACTOR = HEAD_SIZE ** (-0.5)
EXP2_FACTOR = FACTOR * 1.4426950408889634
MASKED = -1e30
BF16 = jnp.bfloat16
F32 = jnp.float32

SMEM = pl.BlockSpec(memory_space=pltpu.SMEM)
VMEM = pl.BlockSpec(memory_space=pltpu.VMEM)
HBM = pl.BlockSpec(memory_space=pl.ANY)
PARAMS = pltpu.CompilerParams(vmem_limit_bytes=28 * 1024 * 1024)


def in_hbm(array):
    return pltpu.with_memory_space_constraint(array, pltpu.HBM)


def in_vmem(array):
    return pltpu.with_memory_space_constraint(array, pltpu.VMEM)


def iota(shape, axis):
    return lax.broadcasted_iota(jnp.int32, shape, axis)


def onehot(hit):
    return jnp.where(hit, 1.0, 0.0).astype(BF16)


def pick(matrix, rows):
    return jnp.dot(matrix, rows, preferred_element_type=F32).astype(BF16)


def part(h, first, width, whole):
    return pl.ds(pl.multiple_of(h * whole + first, HEAD_SIZE), width)


def lanes(width):
    return iota((1, width), 1)


def matching(value, keys, results):
    found = jnp.full_like(value, -1)
    for key, result in zip(keys, results):
        found = jnp.where(value == key, result, found)
    return found


def rows_at(block, place):
    return jnp.where(block >= 0, block * BLOCK + (place & 7), -1)


def placing(target, count):
    return onehot(target == iota((count, target.shape[1]), 0))


def choose_sent(mate, slot):
    place = lanes(ROWS)
    return placing(rows_at(matching(place >> 3, slot, mate), place), ROWS)


def choose_landed(mate, slot):
    place = lanes(ROWS)
    return placing(rows_at(matching(place >> 3, mate, slot), place), ROWS)


def choose_turns(mate):
    place = lanes(ROWS)
    return placing(rows_at(matching(place >> 3, mate, range(ROUNDS)), place), HALF)


def choose_sent_turns(mate):
    place = lanes(HALF)
    return placing(rows_at(matching(place >> 3, range(ROUNDS), mate), place), ROWS)


def packed_row(slot):
    place = lanes(ROWS)
    block = place >> 3
    turn = matching(block, slot, range(ROUNDS))
    lower = jnp.zeros_like(place)
    for t in range(ROUNDS):
        lower = lower + jnp.where(block > slot[t], 1, 0)
    return jnp.where(turn >= 0, HALF + turn * BLOCK, (block - lower) * BLOCK) + (place & 7)


def packing(slot, count=ROWS):
    return placing(packed_row(slot), count)


def unpacking(slot):
    hit = jnp.where(packed_row(slot) == iota((ROWS, ROWS), 0), 1.0, 0.0)
    return hit.T.astype(BF16)


def share_landed(matrix):
    return jnp.broadcast_to(jnp.sum(matrix.astype(F32), axis=1, keepdims=True), (ROWS, HEAD_SIZE))


def replaced(came, landed, own):
    mask = jnp.concatenate([came] * (own.shape[1] // HEAD_SIZE), axis=1)
    return jnp.where(mask > 0.5, landed, own.astype(F32)).astype(BF16)


def scalars(ref, first, count):
    return [ref[first + t] for t in range(count)]


def staying_kernel(slot_ref, k_hbm, v_hbm, stay_ref, k_ref, v_ref, arrived):
    copies = [pltpu.make_async_copy(k_hbm, k_ref, arrived.at[0]), pltpu.make_async_copy(v_hbm, v_ref, arrived.at[1])]
    for copy in copies:
        copy.start()
    keep = packing(scalars(slot_ref, 0, ROUNDS), HALF)
    for copy in copies:
        copy.wait()
    for h in range(KEY_VALUE_HEADS):
        head = part(h, 0, HEAD_SIZE, HEAD_SIZE)
        stay_ref[:, part(h, 0, PAIR, PAIR)] = pick(keep, jnp.concatenate([k_ref[:, head], v_ref[:, head]], axis=1))


def staying(slot, k, v):
    return pl.pallas_call(
        staying_kernel,
        in_specs=[SMEM, HBM, HBM],
        out_specs=VMEM,
        out_shape=pltpu.VMEM((HALF, KEY_VALUE_HEADS * PAIR), BF16),
        scratch_shapes=[pltpu.VMEM(k.shape, BF16), pltpu.VMEM(v.shape, BF16), pltpu.SemaphoreType.DMA((2,))],
        compiler_params=PARAMS,
        cost_estimate=pl.CostEstimate(flops=10**8, bytes_accessed=10**6, transcendentals=0),
        name="staying",
    )(slot, in_hbm(k), in_hbm(v))


def outgoing_kernel(mate_ref, slot_ref, q_ref, k_ref, v_ref, g_ref, send_ref, choose):
    @pl.when(pl.program_id(0) == 0)
    def _():
        choose[...] = choose_sent(scalars(mate_ref, 0, ROUNDS), scalars(slot_ref, 0, ROUNDS))

    rows = jnp.concatenate([q_ref[...], k_ref[...], v_ref[...], g_ref[...]], axis=1)
    send_ref[...] = pick(choose[...], rows)


def outgoing(mate, slot, q, k, v, g):
    wide = pl.BlockSpec((ROWS, WIDE), lambda h: (0, h))
    head = pl.BlockSpec((ROWS, HEAD_SIZE), lambda h: (0, h))
    return pl.pallas_call(
        outgoing_kernel,
        grid=(KEY_VALUE_HEADS,),
        in_specs=[SMEM, SMEM, wide, head, head, wide],
        out_specs=pl.BlockSpec((ROWS, CARGO), lambda h: (0, h)),
        out_shape=pltpu.HBM((ROWS, KEY_VALUE_HEADS * CARGO), BF16),
        scratch_shapes=[pltpu.VMEM((ROWS, ROWS), BF16)],
        compiler_params=PARAMS,
        cost_estimate=pl.CostEstimate(flops=10**9, bytes_accessed=5 * 10**6, transcendentals=0),
        name="outgoing",
    )(mate, slot, in_hbm(q), in_hbm(k), in_hbm(v), in_hbm(g))


def traded_pairs_kernel(mate_ref, landed_ref, out_ref):
    choose = choose_turns(scalars(mate_ref, 0, ROUNDS))
    for h in range(KEY_VALUE_HEADS):
        out_ref[:, part(h, 0, PAIR, PAIR)] = pick(choose, landed_ref[:, part(h, WIDE, PAIR, CARGO)])


def traded_pairs(mate, landed):
    return pl.pallas_call(
        traded_pairs_kernel,
        in_specs=[SMEM, VMEM],
        out_specs=VMEM,
        out_shape=pltpu.VMEM((HALF, KEY_VALUE_HEADS * PAIR), BF16),
        compiler_params=PARAMS,
        cost_estimate=pl.CostEstimate(flops=10**8, bytes_accessed=8 * 10**5, transcendentals=0),
        name="traded_pairs",
    )(mate, in_vmem(landed))


def to_column(row):
    here = iota((ROWS, ROWS), 0) == iota((ROWS, ROWS), 1)
    return jnp.sum(jnp.where(here, row, 0.0), axis=1, keepdims=True)


def earlier_blocks(metas, rank):
    first = metas[0][0]
    count = jnp.int32(0)
    for x in (1, 2, 3):
        for last in range(KEYS - 1, ROWS, KEYS):
            count = count + jnp.where(((rank ^ x) < rank) & (metas[x][last] == first), 1, 0)
    return count


def fill_mask(mask, metas_ids, rank):
    ids = [piece[:, :ROWS].astype(F32) for piece in metas_ids]
    for x in range(RANKS):
        allowed = to_column(ids[x]) == ids[0]
        if x == 0:
            allowed = allowed & (iota((ROWS, 1), 0) <= lanes(ROWS))
        mask[pl.ds(pl.multiple_of((rank ^ x) * ROWS, ROWS), ROWS), :] = jnp.where(allowed, 0.0, MASKED)


INNER = (((1,), (1,)), ((), ()))


def forward_kernel(
    mate_ref, meta_own, meta_near, meta_far, meta_both, ids_own, ids_near, ids_far, ids_both,
    q_hbm, g_hbm, landed_ref, stay_own, stay_near, stay_far, stay_both, turn_own, turn_near, turn_far, turn_both,
    out_hbm, send_hbm, q_kept, g_kept, pairs_kept, stats_hbm,
    out_ref, send_ref, q_ref, g_ref, pairs_ref, stats_ref, bring, place, mask, came, q_arrived, g_arrived, left,
):
    q_copy = pltpu.make_async_copy(q_hbm, q_ref, q_arrived)
    g_copy = pltpu.make_async_copy(g_hbm, g_ref, g_arrived)
    q_copy.start()
    g_copy.start()
    metas = (meta_own, meta_near, meta_far, meta_both)
    rank = metas[0][ROWS + ROUNDS]
    count = earlier_blocks(metas, rank)
    mate, slot = scalars(mate_ref, 0, ROUNDS), scalars(metas[0], ROWS, ROUNDS)
    choose = choose_sent(mate, slot)
    bring[...] = choose_landed(mate, slot)
    came[...] = share_landed(bring[...])
    fill_mask(mask, (ids_own, ids_near, ids_far, ids_both), rank)
    stay = (stay_own, stay_near, stay_far, stay_both)
    turn = (turn_own, turn_near, turn_far, turn_both)
    for x in range(RANKS):
        other = rank ^ x

        @pl.when((other <= rank) & ((rank - other - 1) * ROWS < count * KEYS))
        def _(x=x, other=other):
            rows = jnp.concatenate([stay[x][...], turn[x][...]], axis=0)
            place[...] = unpacking(scalars(metas[x], ROWS, ROUNDS))
            pairs_ref[pl.ds(pl.multiple_of(other * ROWS, ROWS), ROWS), :] = pick(place[...], rows)

    q_copy.wait()
    g_copy.wait()

    def leave(h, turn, source, target, whole):
        columns = part(h, 0, whole, whole)
        return pltpu.make_async_copy(source.at[:, columns], target.at[:, columns], left.at[turn, h])

    def leave_early(h):
        return [leave(h, 0, q_ref, q_kept, WIDE), leave(h, 1, g_ref, g_kept, WIDE), leave(h, 2, pairs_ref, pairs_kept, PAIR)]

    def leave_late(h):
        return [leave(h, 3, out_ref, out_hbm, WIDE), leave(h, 4, send_ref, send_hbm, WIDE)]

    def head(h, carry):
        wide = part(h, 0, WIDE, WIDE)
        came_q = jnp.dot(bring[...], landed_ref[:, part(h, 0, WIDE, CARGO)], preferred_element_type=F32)
        came_g = jnp.dot(bring[...], landed_ref[:, part(h, BUNDLE, WIDE, CARGO)], preferred_element_type=F32)
        q_ref[:, wide] = replaced(came[...], came_q, q_ref[:, wide])
        g_ref[:, wide] = replaced(came[...], came_g, g_ref[:, wide])
        for copy in leave_early(h):
            copy.start()

        for n in range(EARLIER + 1):

            @pl.when(count == n)
            def _(n=n):
                window = pl.ds(pl.multiple_of(rank * ROWS - n * KEYS, KEYS), n * KEYS + ROWS)
                k = pairs_ref[window, part(h, 0, HEAD_SIZE, PAIR)]
                v_turned = pairs_ref[window, part(h, HEAD_SIZE, HEAD_SIZE, PAIR)].T
                heads = [part(h, i * HEAD_SIZE, HEAD_SIZE, WIDE) for i in range(SHARED)]
                q = jnp.concatenate([q_ref[:, columns] for columns in heads], axis=0)
                g_turned = jnp.concatenate([g_ref[:, columns].T for columns in heads], axis=1)
                logits = lax.dot_general(k, q, INNER, preferred_element_type=F32)
                logits = logits + jnp.concatenate([mask[window, :]] * SHARED, axis=1)
                top = jnp.max(logits, axis=0, keepdims=True)
                raised = jnp.exp2((logits - top) * EXP2_FACTOR)
                total = jnp.sum(raised, axis=0, keepdims=True)
                out = jnp.dot(v_turned, raised.astype(BF16), preferred_element_type=F32) * (1.0 / total)
                inner = jnp.sum(out * g_turned.astype(F32), axis=0, keepdims=True)
                out = out.astype(BF16)
                for i, columns in enumerate(heads):
                    out_ref[:, columns] = out[:, i * ROWS : (i + 1) * ROWS].T
                stats_ref[h] = jnp.concatenate([top * EXP2_FACTOR + jnp.log2(total), inner], axis=0)

        send_ref[:, wide] = pick(choose, out_ref[:, wide])
        for copy in leave_late(h):
            copy.start()
        return carry

    lax.fori_loop(0, KEY_VALUE_HEADS, head, 0)
    stats_copy = pltpu.make_async_copy(stats_ref, stats_hbm, q_arrived)
    stats_copy.start()
    for h in range(KEY_VALUE_HEADS):
        for copy in leave_early(h) + leave_late(h):
            copy.wait()
    stats_copy.wait()


def forward(mate, metas, q, g, landed, stays, turns):
    wide = (ROWS, KEY_VALUE_HEADS * WIDE)
    return pl.pallas_call(
        forward_kernel,
        in_specs=[SMEM] * 5 + [VMEM] * 4 + [HBM] * 2 + [VMEM] * (1 + 2 * RANKS),
        out_specs=[HBM] * 6,
        out_shape=[
            pltpu.HBM(wide, BF16),
            pltpu.HBM(wide, BF16),
            pltpu.HBM(wide, BF16),
            pltpu.HBM(wide, BF16),
            pltpu.HBM((RANKS * ROWS, KEY_VALUE_HEADS * PAIR), BF16),
            pltpu.HBM((KEY_VALUE_HEADS, 2, SHARED * ROWS), F32),
        ],
        scratch_shapes=[
            pltpu.VMEM(wide, BF16),
            pltpu.VMEM(wide, BF16),
            pltpu.VMEM(wide, BF16),
            pltpu.VMEM(wide, BF16),
            pltpu.VMEM((RANKS * ROWS, KEY_VALUE_HEADS * PAIR), BF16),
            pltpu.VMEM((KEY_VALUE_HEADS, 2, SHARED * ROWS), F32),
            pltpu.VMEM((ROWS, ROWS), BF16),
            pltpu.VMEM((ROWS, ROWS), BF16),
            pltpu.VMEM((RANKS * ROWS, ROWS), F32),
            pltpu.VMEM((ROWS, HEAD_SIZE), F32),
            pltpu.SemaphoreType.DMA,
            pltpu.SemaphoreType.DMA,
            pltpu.SemaphoreType.DMA((5, KEY_VALUE_HEADS)),
        ],
        compiler_params=PARAMS,
        cost_estimate=pl.CostEstimate(flops=4 * 10**9, bytes_accessed=10**7, transcendentals=4 * 10**6),
        name="forward",
    )(
        mate, *metas, *[in_vmem(meta.reshape(1, META)) for meta in metas],
        in_hbm(q), in_hbm(g), in_vmem(landed), *[in_vmem(x) for x in (*stays, *turns)],
    )


def backward_kernel(
    mate_ref, meta_own, meta_near, meta_far, meta_both, ids_own, ids_near, ids_far, ids_both,
    q_hbm, g_hbm, pairs_hbm, stats_hbm,
    dq_hbm, send_ref, turn_keep, turn_send, keep_hbm, send_hbm,
    q_ref, g_ref, pairs_ref, stats_ref, dq_ref, stay_keep, stay_send, mask, total, arrived, stats_arrived, left, stay_left,
):
    def arrive(h, turn, source, target, whole):
        columns = part(h, 0, whole, whole)
        return pltpu.make_async_copy(source.at[:, columns], target.at[:, columns], arrived.at[turn, h])

    def arrivals(h):
        return [arrive(h, 0, pairs_hbm, pairs_ref, PAIR), arrive(h, 1, q_hbm, q_ref, WIDE), arrive(h, 2, g_hbm, g_ref, WIDE)]

    stats_copy = pltpu.make_async_copy(stats_hbm, stats_ref, stats_arrived)
    stats_copy.start()
    for h in range(KEY_VALUE_HEADS):
        for copy in arrivals(h):
            copy.start()
    metas = (meta_own, meta_near, meta_far, meta_both)
    rank = metas[0][ROWS + ROUNDS]
    count = earlier_blocks(metas, rank)
    choose = choose_sent(scalars(mate_ref, 0, ROUNDS), scalars(metas[0], ROWS, ROUNDS))
    fill_mask(mask, (ids_own, ids_near, ids_far, ids_both), rank)
    total[...] = jnp.zeros_like(total)

    def leave(h):
        columns = part(h, 0, WIDE, WIDE)
        return pltpu.make_async_copy(dq_ref.at[:, columns], dq_hbm.at[:, columns], left.at[h])

    stats_copy.wait()

    def head(h, carry):
        for copy in arrivals(h):
            copy.wait()

        for n in range(EARLIER + 1):

            @pl.when(count == n)
            def _(n=n):
                window = pl.ds(pl.multiple_of(rank * ROWS - n * KEYS, KEYS), n * KEYS + ROWS)
                k_columns = part(h, 0, HEAD_SIZE, PAIR)
                v_columns = part(h, HEAD_SIZE, HEAD_SIZE, PAIR)
                k = pairs_ref[window, k_columns]
                v = pairs_ref[window, v_columns]
                k_turned = k.T
                heads = [part(h, i * HEAD_SIZE, HEAD_SIZE, WIDE) for i in range(SHARED)]
                q = jnp.concatenate([q_ref[:, columns] for columns in heads], axis=0)
                g = jnp.concatenate([g_ref[:, columns] for columns in heads], axis=0)
                stats = stats_ref[h]
                logits = lax.dot_general(k, q, INNER, preferred_element_type=F32)
                allowed = jnp.concatenate([mask[window, :]] * SHARED, axis=1)
                weights = jnp.exp2(logits * EXP2_FACTOR - stats[0:1] + allowed)
                grad_weights = lax.dot_general(v, g, INNER, preferred_element_type=F32)
                grad_logits = (weights * (grad_weights - stats[1:2])).astype(BF16)
                dq = (jnp.dot(k_turned, grad_logits, preferred_element_type=F32) * FACTOR).astype(BF16)
                for i, columns in enumerate(heads):
                    dq_ref[:, columns] = dq[:, i * ROWS : (i + 1) * ROWS].T
                dk = jnp.dot(grad_logits, q, preferred_element_type=F32)
                dv = jnp.dot(weights.astype(BF16), g, preferred_element_type=F32)
                total[window, k_columns] = (dk * FACTOR).astype(BF16)
                total[window, v_columns] = dv.astype(BF16)

        leave(h).start()
        wide = part(h, 0, WIDE, WIDE)
        send_ref[:, wide] = pick(choose, dq_ref[:, wide])
        return carry

    lax.fori_loop(0, KEY_VALUE_HEADS, head, 0)
    for x in range(RANKS):
        rows = total[pl.ds(pl.multiple_of((rank ^ x) * ROWS, ROWS), ROWS), :]
        pieces = pick(packing(scalars(metas[x], ROWS, ROUNDS)), rows)
        stay, turn = ((stay_keep, turn_keep), (stay_send, turn_send))[x & 1]
        stay[x >> 1] = pieces[:HALF]
        turn[x >> 1] = pieces[HALF:]
    leaving = [
        pltpu.make_async_copy(stay_keep, keep_hbm, stay_left.at[0]),
        pltpu.make_async_copy(stay_send, send_hbm, stay_left.at[1]),
    ]
    for copy in leaving:
        copy.start()
    for copy in leaving + [leave(h) for h in range(KEY_VALUE_HEADS)]:
        copy.wait()


def backward(mate, metas, q, g, pairs, stats):
    wide = (ROWS, KEY_VALUE_HEADS * WIDE)
    piece = (2, HALF, KEY_VALUE_HEADS * PAIR)
    return pl.pallas_call(
        backward_kernel,
        in_specs=[SMEM] * 5 + [VMEM] * 4 + [HBM] * 4,
        out_specs=[HBM, VMEM, VMEM, VMEM, HBM, HBM],
        out_shape=[
            pltpu.HBM(wide, BF16),
            pltpu.VMEM(wide, BF16),
            pltpu.VMEM(piece, BF16),
            pltpu.VMEM(piece, BF16),
            pltpu.HBM(piece, BF16),
            pltpu.HBM(piece, BF16),
        ],
        scratch_shapes=[
            pltpu.VMEM(wide, BF16),
            pltpu.VMEM(wide, BF16),
            pltpu.VMEM(pairs.shape, BF16),
            pltpu.VMEM(stats.shape, F32),
            pltpu.VMEM(wide, BF16),
            pltpu.VMEM(piece, BF16),
            pltpu.VMEM(piece, BF16),
            pltpu.VMEM((RANKS * ROWS, ROWS), F32),
            pltpu.VMEM(pairs.shape, BF16),
            pltpu.SemaphoreType.DMA((3, KEY_VALUE_HEADS)),
            pltpu.SemaphoreType.DMA,
            pltpu.SemaphoreType.DMA((KEY_VALUE_HEADS,)),
            pltpu.SemaphoreType.DMA((2,)),
        ],
        compiler_params=PARAMS,
        cost_estimate=pl.CostEstimate(flops=8 * 10**9, bytes_accessed=10**7, transcendentals=4 * 10**6),
        name="backward",
    )(
        mate, *metas, *[in_vmem(meta.reshape(1, META)) for meta in metas],
        in_hbm(q), in_hbm(g), in_hbm(pairs), in_hbm(stats),
    )


def returning_kernel(mate_ref, dq_ref, own_ref, near_ref, far_ref, send_ref):
    choose = choose_sent_turns(scalars(mate_ref, 0, ROUNDS))
    for h in range(KEY_VALUE_HEADS):
        columns = part(h, 0, PAIR, PAIR)
        total = (
            own_ref[0, :, columns].astype(F32) + near_ref[0, :, columns].astype(F32) + far_ref[:, columns].astype(F32)
        )
        send_ref[:, part(h, 0, WIDE, BUNDLE)] = dq_ref[:, part(h, 0, WIDE, WIDE)]
        send_ref[:, part(h, WIDE, PAIR, BUNDLE)] = pick(choose, total.astype(BF16))


def returning(mate, dq, own, near, far):
    return pl.pallas_call(
        returning_kernel,
        in_specs=[SMEM] + [VMEM] * 4,
        out_specs=VMEM,
        out_shape=pltpu.VMEM((ROWS, KEY_VALUE_HEADS * BUNDLE), BF16),
        compiler_params=PARAMS,
        cost_estimate=pl.CostEstimate(flops=10**8, bytes_accessed=10**6, transcendentals=0),
        name="returning",
    )(mate, in_vmem(dq), in_vmem(own), in_vmem(near), in_vmem(far))


def merge_kernel(mate_ref, slot_ref, own_ref, landed_ref, out_ref, bring, came):
    @pl.when(pl.program_id(0) == 0)
    def _():
        bring[...] = choose_landed(scalars(mate_ref, 0, ROUNDS), scalars(slot_ref, 0, ROUNDS))
        came[...] = share_landed(bring[...])

    landed = jnp.dot(bring[...], landed_ref[...], preferred_element_type=F32)
    out_ref[...] = replaced(came[...], landed, own_ref[...])


def merge(mate, slot, own, landed):
    wide = pl.BlockSpec((ROWS, WIDE), lambda h: (0, h))
    return pl.pallas_call(
        merge_kernel,
        grid=(KEY_VALUE_HEADS,),
        in_specs=[SMEM, SMEM, wide, wide],
        out_specs=wide,
        out_shape=pltpu.HBM(own.shape, BF16),
        scratch_shapes=[pltpu.VMEM((ROWS, ROWS), BF16), pltpu.VMEM((ROWS, HEAD_SIZE), F32)],
        compiler_params=PARAMS,
        cost_estimate=pl.CostEstimate(flops=5 * 10**8, bytes_accessed=3 * 10**6, transcendentals=0),
        name="merge",
    )(mate, slot, in_hbm(own), in_vmem(landed))


def finish_kernel(
    mate_ref, slot_ref, dq_hbm, landed_ref, own_hbm, near_ref, far_ref,
    grad_q, grad_k, grad_v,
    dq_ref, own_ref, k_ref, v_ref, arrived, left,
):
    own_arriving = pltpu.make_async_copy(own_hbm, own_ref, arrived.at[1])
    own_arriving.start()
    arriving = pltpu.make_async_copy(dq_hbm, dq_ref, arrived.at[0])
    arriving.start()
    mate, slot = scalars(mate_ref, 0, ROUNDS), scalars(slot_ref, 0, ROUNDS)
    bring = choose_landed(mate, slot)
    came = share_landed(bring)
    place = unpacking(slot)[:, :HALF]
    own_arriving.wait()
    for h in range(KEY_VALUE_HEADS):
        columns = part(h, 0, PAIR, PAIR)
        total = (
            own_ref[0, :, columns].astype(F32) + near_ref[0, :, columns].astype(F32) + far_ref[:, columns].astype(F32)
        )
        landed = jnp.dot(bring, landed_ref[:, part(h, WIDE, PAIR, BUNDLE)], preferred_element_type=F32)
        pairs = (jnp.dot(place, total.astype(BF16), preferred_element_type=F32) + landed).astype(BF16)
        k_ref[:, part(h, 0, HEAD_SIZE, HEAD_SIZE)] = pairs[:, :HEAD_SIZE]
        v_ref[:, part(h, 0, HEAD_SIZE, HEAD_SIZE)] = pairs[:, HEAD_SIZE:]
    leaving = [
        pltpu.make_async_copy(k_ref, grad_k, left.at[0]),
        pltpu.make_async_copy(v_ref, grad_v, left.at[1]),
    ]
    for copy in leaving:
        copy.start()
    arriving.wait()
    for h in range(KEY_VALUE_HEADS):
        columns = part(h, 0, WIDE, WIDE)
        landed = jnp.dot(bring, landed_ref[:, part(h, 0, WIDE, BUNDLE)], preferred_element_type=F32)
        dq_ref[:, columns] = replaced(came, landed, dq_ref[:, columns])
        copy = pltpu.make_async_copy(dq_ref.at[:, columns], grad_q.at[:, columns], left.at[2 + h])
        copy.start()
        leaving.append(copy)
    for copy in leaving:
        copy.wait()


def finish(mate, slot, dq, landed, own, near, far):
    narrow = (ROWS, KEY_VALUE_HEADS * HEAD_SIZE)
    return pl.pallas_call(
        finish_kernel,
        in_specs=[SMEM, SMEM, HBM, VMEM, HBM, VMEM, VMEM],
        out_specs=[HBM] * 3,
        out_shape=[pltpu.HBM(dq.shape, BF16), pltpu.HBM(narrow, BF16), pltpu.HBM(narrow, BF16)],
        scratch_shapes=[
            pltpu.VMEM(dq.shape, BF16),
            pltpu.VMEM(own.shape, BF16),
            pltpu.VMEM(narrow, BF16),
            pltpu.VMEM(narrow, BF16),
            pltpu.SemaphoreType.DMA((2,)),
            pltpu.SemaphoreType.DMA((2 + KEY_VALUE_HEADS,)),
        ],
        compiler_params=PARAMS,
        cost_estimate=pl.CostEstimate(flops=8 * 10**8, bytes_accessed=5 * 10**6, transcendentals=0),
        name="finish",
    )(mate, slot, in_hbm(dq), in_vmem(landed), in_hbm(own), in_vmem(near), in_vmem(far))


def exchange(rows):
    blocks = rows.reshape(GROUPS, BLOCK, rows.shape[-1])
    return lax.all_to_all(blocks, "dp", split_axis=0, concat_axis=0, tiled=True).reshape(rows.shape)


def across(array):
    return lax.ppermute(array, "sp", [(i, i ^ 2) for i in range(RANKS)])


def beside(array):
    return lax.ppermute(array, "sp", [(i, i ^ 1) for i in range(RANKS)])


def spread(array):
    far = across(array)
    return array, beside(array), far, beside(far)


def partial_sum(keep, near):
    return (keep[1].astype(F32) + near[1].astype(F32)).astype(BF16)


def body(queries, keys, values, cotangent, doc_ids, partners, swap_slots):
    q, k, v, g = queries[0], keys[0], values[0], cotangent[0]
    mate = in_hbm(partners.reshape(ROUNDS))
    slots = swap_slots.reshape(ROUNDS)
    slot = in_hbm(slots)
    rank = lax.axis_index("sp").astype(jnp.int32).reshape(1)
    meta = jnp.concatenate(
        [doc_ids.reshape(ROWS), slots, rank, jnp.zeros((META - ROWS - ROUNDS - 1,), jnp.int32)]
    )

    stay = staying(slot, k, v)
    stay_far = across(stay)
    send = outgoing(mate, slot, q, k, v, g)
    send, stay_far = lax.optimization_barrier((send, stay_far))
    landed = exchange(send)
    stays = stay, beside(stay), stay_far, beside(stay_far)
    metas = meta, beside(meta), across(meta), lax.ppermute(meta, "sp", [(i, i ^ 3) for i in range(RANKS)])
    landed, stays, metas = lax.optimization_barrier((landed, stays, metas))
    turns = spread(traded_pairs(mate, landed))
    out, send, *kept = forward(mate, metas, q, g, landed, stays, turns)
    landed_out = exchange(send)
    dq, send, turn_keep, turn_send, stay_keep, stay_send = backward(mate, metas, *kept)
    landed_out, turn_send = lax.optimization_barrier((landed_out, turn_send))
    turn_near = beside(turn_send)
    turn_far = across(partial_sum(turn_keep, turn_near))
    stay_near = beside(stay_send)
    stay_far = across(partial_sum(stay_keep, stay_near))
    send = returning(mate, send, turn_keep, turn_near, turn_far)
    send, stay_far = lax.optimization_barrier((send, stay_far))
    landed = exchange(send)
    attended = merge(mate, slot, out, landed_out)
    grad_q, grad_k, grad_v = finish(mate, slot, dq, landed, stay_keep, stay_near, stay_far)
    return attended[None], grad_q[None], grad_k[None], grad_v[None]


def solution(mesh):
    rows = P("dp", "sp", None)
    return jax.shard_map(
        body,
        mesh=mesh,
        in_specs=(rows, rows, rows, rows, P("dp", "sp"), P(None, "dp"), rows),
        out_specs=(rows, rows, rows, rows),
        check_vma=False,
    )
```

```python
import jax
import jax.numpy as jnp
from jax import lax
from jax.experimental import pallas as pl
from jax.experimental.pallas import tpu as pltpu
from jax.sharding import PartitionSpec as P

KEY_VALUE_HEADS = 4
SHARED = 4
HEAD_SIZE = 128
BLOCK = 8
ROUNDS = 16
ROWS = 256
HALF = ROUNDS * BLOCK
GROUPS = 32
RANKS = 4
WIDE = SHARED * HEAD_SIZE
PAIR = 2 * HEAD_SIZE
BUNDLE = WIDE + PAIR
CARGO = 2 * WIDE + PAIR
META = 384
KEYS = 128
TOGETHER = 2
EARLIER = (RANKS - 1) * ROWS // KEYS
FACTOR = HEAD_SIZE ** (-0.5)
EXP2_FACTOR = FACTOR * 1.4426950408889634
MASKED = -1e30
BF16 = jnp.bfloat16
F32 = jnp.float32

SMEM = pl.BlockSpec(memory_space=pltpu.SMEM)
VMEM = pl.BlockSpec(memory_space=pltpu.VMEM)
HBM = pl.BlockSpec(memory_space=pl.ANY)
PARAMS = pltpu.CompilerParams(vmem_limit_bytes=28 * 1024 * 1024)


def in_hbm(array):
    return pltpu.with_memory_space_constraint(array, pltpu.HBM)


def in_vmem(array):
    return pltpu.with_memory_space_constraint(array, pltpu.VMEM)


def iota(shape, axis):
    return lax.broadcasted_iota(jnp.int32, shape, axis)


def onehot(hit):
    return jnp.where(hit, 1.0, 0.0).astype(BF16)


def pick(matrix, rows):
    return jnp.dot(matrix, rows, preferred_element_type=F32).astype(BF16)


def part(h, first, width, whole):
    return pl.ds(pl.multiple_of(h * whole + first, HEAD_SIZE), width)


def lanes(width):
    return iota((1, width), 1)


def matching(value, keys, results):
    found = jnp.full_like(value, -1)
    for key, result in zip(keys, results):
        found = jnp.where(value == key, result, found)
    return found


def rows_at(block, place):
    return jnp.where(block >= 0, block * BLOCK + (place & 7), -1)


def placing(target, count):
    return onehot(target == iota((count, target.shape[1]), 0))


def choose_sent(mate, slot):
    place = lanes(ROWS)
    return placing(rows_at(matching(place >> 3, slot, mate), place), ROWS)


def choose_landed(mate, slot):
    place = lanes(ROWS)
    return placing(rows_at(matching(place >> 3, mate, slot), place), ROWS)


def choose_turns(mate):
    place = lanes(ROWS)
    return placing(rows_at(matching(place >> 3, mate, range(ROUNDS)), place), HALF)


def choose_sent_turns(mate):
    place = lanes(HALF)
    return placing(rows_at(matching(place >> 3, range(ROUNDS), mate), place), ROWS)


def packed_row(slot):
    place = lanes(ROWS)
    block = place >> 3
    turn = matching(block, slot, range(ROUNDS))
    lower = jnp.zeros_like(place)
    for t in range(ROUNDS):
        lower = lower + jnp.where(block > slot[t], 1, 0)
    return jnp.where(turn >= 0, HALF + turn * BLOCK, (block - lower) * BLOCK) + (place & 7)


def packing(slot, count=ROWS):
    return placing(packed_row(slot), count)


def unpacking(slot):
    hit = jnp.where(packed_row(slot) == iota((ROWS, ROWS), 0), 1.0, 0.0)
    return hit.T.astype(BF16)


def share_landed(matrix):
    return jnp.broadcast_to(jnp.sum(matrix.astype(F32), axis=1, keepdims=True), (ROWS, HEAD_SIZE))


def replaced(came, landed, own):
    mask = jnp.concatenate([came] * (own.shape[1] // HEAD_SIZE), axis=1)
    return jnp.where(mask > 0.5, landed, own.astype(F32)).astype(BF16)


def scalars(ref, first, count):
    return [ref[first + t] for t in range(count)]


def staying_kernel(slot_ref, k_hbm, v_hbm, stay_ref, k_ref, v_ref, arrived):
    copies = [pltpu.make_async_copy(k_hbm, k_ref, arrived.at[0]), pltpu.make_async_copy(v_hbm, v_ref, arrived.at[1])]
    for copy in copies:
        copy.start()
    keep = packing(scalars(slot_ref, 0, ROUNDS), HALF)
    for copy in copies:
        copy.wait()
    for h in range(KEY_VALUE_HEADS):
        head = part(h, 0, HEAD_SIZE, HEAD_SIZE)
        stay_ref[:, part(h, 0, PAIR, PAIR)] = pick(keep, jnp.concatenate([k_ref[:, head], v_ref[:, head]], axis=1))


def staying(slot, k, v):
    return pl.pallas_call(
        staying_kernel,
        in_specs=[SMEM, HBM, HBM],
        out_specs=VMEM,
        out_shape=pltpu.VMEM((HALF, KEY_VALUE_HEADS * PAIR), BF16),
        scratch_shapes=[pltpu.VMEM(k.shape, BF16), pltpu.VMEM(v.shape, BF16), pltpu.SemaphoreType.DMA((2,))],
        compiler_params=PARAMS,
        cost_estimate=pl.CostEstimate(flops=10**8, bytes_accessed=10**6, transcendentals=0),
        name="staying",
    )(slot, in_hbm(k), in_hbm(v))


def outgoing_kernel(mate_ref, slot_ref, q_ref, k_ref, v_ref, g_ref, send_ref, choose):
    @pl.when(pl.program_id(0) == 0)
    def _():
        choose[...] = choose_sent(scalars(mate_ref, 0, ROUNDS), scalars(slot_ref, 0, ROUNDS))

    rows = jnp.concatenate([q_ref[...], k_ref[...], v_ref[...], g_ref[...]], axis=1)
    send_ref[...] = pick(choose[...], rows)


def outgoing(mate, slot, q, k, v, g):
    wide = pl.BlockSpec((ROWS, WIDE), lambda h: (0, h))
    head = pl.BlockSpec((ROWS, HEAD_SIZE), lambda h: (0, h))
    return pl.pallas_call(
        outgoing_kernel,
        grid=(KEY_VALUE_HEADS,),
        in_specs=[SMEM, SMEM, wide, head, head, wide],
        out_specs=pl.BlockSpec((ROWS, CARGO), lambda h: (0, h)),
        out_shape=pltpu.HBM((ROWS, KEY_VALUE_HEADS * CARGO), BF16),
        scratch_shapes=[pltpu.VMEM((ROWS, ROWS), BF16)],
        compiler_params=PARAMS,
        cost_estimate=pl.CostEstimate(flops=10**9, bytes_accessed=5 * 10**6, transcendentals=0),
        name="outgoing",
    )(mate, slot, in_hbm(q), in_hbm(k), in_hbm(v), in_hbm(g))


def traded_pairs_kernel(mate_ref, landed_ref, out_ref):
    choose = choose_turns(scalars(mate_ref, 0, ROUNDS))
    for h in range(KEY_VALUE_HEADS):
        out_ref[:, part(h, 0, PAIR, PAIR)] = pick(choose, landed_ref[:, part(h, WIDE, PAIR, CARGO)])


def traded_pairs(mate, landed):
    return pl.pallas_call(
        traded_pairs_kernel,
        in_specs=[SMEM, VMEM],
        out_specs=VMEM,
        out_shape=pltpu.VMEM((HALF, KEY_VALUE_HEADS * PAIR), BF16),
        compiler_params=PARAMS,
        cost_estimate=pl.CostEstimate(flops=10**8, bytes_accessed=8 * 10**5, transcendentals=0),
        name="traded_pairs",
    )(mate, in_vmem(landed))


def to_column(row):
    here = iota((ROWS, ROWS), 0) == iota((ROWS, ROWS), 1)
    return jnp.sum(jnp.where(here, row, 0.0), axis=1, keepdims=True)


def earlier_blocks(metas, rank, keys):
    first = metas[0][0]
    count = jnp.int32(0)
    for x in (1, 2, 3):
        for last in range(keys - 1, ROWS, keys):
            count = count + jnp.where(((rank ^ x) < rank) & (metas[x][last] == first), 1, 0)
    return count


def fill_mask(mask, metas_ids, rank):
    ids = [piece[:, :ROWS].astype(F32) for piece in metas_ids]
    for x in range(RANKS):
        allowed = to_column(ids[x]) == ids[0]
        if x == 0:
            allowed = allowed & (iota((ROWS, 1), 0) <= lanes(ROWS))
        mask[pl.ds(pl.multiple_of((rank ^ x) * ROWS, ROWS), ROWS), :] = jnp.where(allowed, 0.0, MASKED)


INNER = (((1,), (1,)), ((), ()))


def forward_kernel(
    mate_ref, meta_own, meta_near, meta_far, meta_both, ids_own, ids_near, ids_far, ids_both,
    q_hbm, g_hbm, landed_ref, stay_own, stay_near, stay_far, stay_both, turn_own, turn_near, turn_far, turn_both,
    out_hbm, send_hbm, q_kept, g_kept, pairs_kept, stats_hbm,
    out_ref, send_ref, q_ref, g_ref, pairs_ref, stats_ref, bring, place, mask, came, q_arrived, g_arrived, left,
):
    q_copy = pltpu.make_async_copy(q_hbm, q_ref, q_arrived)
    g_copy = pltpu.make_async_copy(g_hbm, g_ref, g_arrived)
    q_copy.start()
    g_copy.start()
    metas = (meta_own, meta_near, meta_far, meta_both)
    rank = metas[0][ROWS + ROUNDS]
    count = earlier_blocks(metas, rank, ROWS)
    mate, slot = scalars(mate_ref, 0, ROUNDS), scalars(metas[0], ROWS, ROUNDS)
    choose = choose_sent(mate, slot)
    bring[...] = choose_landed(mate, slot)
    came[...] = share_landed(bring[...])
    fill_mask(mask, (ids_own, ids_near, ids_far, ids_both), rank)
    stay = (stay_own, stay_near, stay_far, stay_both)
    turn = (turn_own, turn_near, turn_far, turn_both)
    for x in range(RANKS):
        other = rank ^ x

        @pl.when((other <= rank) & (rank - other <= count))
        def _(x=x, other=other):
            rows = jnp.concatenate([stay[x][...], turn[x][...]], axis=0)
            place[...] = unpacking(scalars(metas[x], ROWS, ROUNDS))
            pairs_ref[pl.ds(pl.multiple_of(other * ROWS, ROWS), ROWS), :] = pick(place[...], rows)

    q_copy.wait()
    g_copy.wait()

    def leave(h, turn, source, target, whole):
        columns = part(h, 0, whole, whole)
        return pltpu.make_async_copy(source.at[:, columns], target.at[:, columns], left.at[turn, h])

    def leave_early(h):
        return [leave(h, 0, q_ref, q_kept, WIDE), leave(h, 1, g_ref, g_kept, WIDE), leave(h, 2, pairs_ref, pairs_kept, PAIR)]

    def leave_late(h):
        return [leave(h, 3, out_ref, out_hbm, WIDE), leave(h, 4, send_ref, send_hbm, WIDE)]

    def merged(h):
        wide = part(h, 0, WIDE, WIDE)
        came_q = jnp.dot(bring[...], landed_ref[:, part(h, 0, WIDE, CARGO)], preferred_element_type=F32)
        came_g = jnp.dot(bring[...], landed_ref[:, part(h, BUNDLE, WIDE, CARGO)], preferred_element_type=F32)
        q_ref[:, wide] = replaced(came[...], came_q, q_ref[:, wide])
        g_ref[:, wide] = replaced(came[...], came_g, g_ref[:, wide])
        for copy in leave_early(h):
            copy.start()

    def attend(h, n):
        window = pl.ds(pl.multiple_of(rank * ROWS - n * ROWS, ROWS), n * ROWS + ROWS)
        k = pairs_ref[window, part(h, 0, HEAD_SIZE, PAIR)]
        v_turned = pairs_ref[window, part(h, HEAD_SIZE, HEAD_SIZE, PAIR)].T
        heads = [part(h, i * HEAD_SIZE, HEAD_SIZE, WIDE) for i in range(SHARED)]
        q = jnp.concatenate([q_ref[:, columns] for columns in heads], axis=0)
        g_turned = jnp.concatenate([g_ref[:, columns].T for columns in heads], axis=1)
        logits = lax.dot_general(k, q, INNER, preferred_element_type=F32)
        logits = logits + jnp.concatenate([mask[window, :]] * SHARED, axis=1)
        top = jnp.max(logits, axis=0, keepdims=True)
        raised = jnp.exp2((logits - top) * EXP2_FACTOR)
        total = jnp.sum(raised, axis=0, keepdims=True)
        out = jnp.dot(v_turned, raised.astype(BF16), preferred_element_type=F32) * (1.0 / total)
        inner = jnp.sum(out * g_turned.astype(F32), axis=0, keepdims=True)
        out = out.astype(BF16)
        for i, columns in enumerate(heads):
            out_ref[:, columns] = out[:, i * ROWS : (i + 1) * ROWS].T
        stats_ref[h] = jnp.concatenate([top * EXP2_FACTOR + jnp.log2(total), inner], axis=0)

    def sent(h):
        wide = part(h, 0, WIDE, WIDE)
        send_ref[:, wide] = pick(choose, out_ref[:, wide])
        for copy in leave_late(h):
            copy.start()

    def heads_at(step, carry):
        heads = [step * TOGETHER + i for i in range(TOGETHER)]
        for h in heads:
            merged(h)
        for n in range(RANKS):

            @pl.when(count == n)
            def _(n=n):
                for h in heads:
                    attend(h, n)

        for h in heads:
            sent(h)
        return carry

    lax.fori_loop(0, KEY_VALUE_HEADS // TOGETHER, heads_at, 0)
    stats_copy = pltpu.make_async_copy(stats_ref, stats_hbm, q_arrived)
    stats_copy.start()
    for h in range(KEY_VALUE_HEADS):
        for copy in leave_early(h) + leave_late(h):
            copy.wait()
    stats_copy.wait()


def forward(mate, metas, q, g, landed, stays, turns):
    wide = (ROWS, KEY_VALUE_HEADS * WIDE)
    return pl.pallas_call(
        forward_kernel,
        in_specs=[SMEM] * 5 + [VMEM] * 4 + [HBM] * 2 + [VMEM] * (1 + 2 * RANKS),
        out_specs=[HBM] * 6,
        out_shape=[
            pltpu.HBM(wide, BF16),
            pltpu.HBM(wide, BF16),
            pltpu.HBM(wide, BF16),
            pltpu.HBM(wide, BF16),
            pltpu.HBM((RANKS * ROWS, KEY_VALUE_HEADS * PAIR), BF16),
            pltpu.HBM((KEY_VALUE_HEADS, 2, SHARED * ROWS), F32),
        ],
        scratch_shapes=[
            pltpu.VMEM(wide, BF16),
            pltpu.VMEM(wide, BF16),
            pltpu.VMEM(wide, BF16),
            pltpu.VMEM(wide, BF16),
            pltpu.VMEM((RANKS * ROWS, KEY_VALUE_HEADS * PAIR), BF16),
            pltpu.VMEM((KEY_VALUE_HEADS, 2, SHARED * ROWS), F32),
            pltpu.VMEM((ROWS, ROWS), BF16),
            pltpu.VMEM((ROWS, ROWS), BF16),
            pltpu.VMEM((RANKS * ROWS, ROWS), F32),
            pltpu.VMEM((ROWS, HEAD_SIZE), F32),
            pltpu.SemaphoreType.DMA,
            pltpu.SemaphoreType.DMA,
            pltpu.SemaphoreType.DMA((5, KEY_VALUE_HEADS)),
        ],
        compiler_params=PARAMS,
        cost_estimate=pl.CostEstimate(flops=4 * 10**9, bytes_accessed=10**7, transcendentals=4 * 10**6),
        name="forward",
    )(
        mate, *metas, *[in_vmem(meta.reshape(1, META)) for meta in metas],
        in_hbm(q), in_hbm(g), in_vmem(landed), *[in_vmem(x) for x in (*stays, *turns)],
    )


def backward_kernel(
    mate_ref, meta_own, meta_near, meta_far, meta_both, ids_own, ids_near, ids_far, ids_both,
    q_hbm, g_hbm, pairs_hbm, stats_hbm,
    dq_hbm, cargo_hbm, turn_keep, turn_send, keep_hbm, send_hbm,
    send_ref, q_ref, g_ref, pairs_ref, stats_ref, dq_ref, stay_keep, stay_send, mask, total, arrived, stats_arrived, left, stay_left,
):
    def arrive(h, turn, source, target, whole):
        columns = part(h, 0, whole, whole)
        return pltpu.make_async_copy(source.at[:, columns], target.at[:, columns], arrived.at[turn, h])

    def arrivals(h):
        return [arrive(h, 0, pairs_hbm, pairs_ref, PAIR), arrive(h, 1, q_hbm, q_ref, WIDE), arrive(h, 2, g_hbm, g_ref, WIDE)]

    stats_copy = pltpu.make_async_copy(stats_hbm, stats_ref, stats_arrived)
    stats_copy.start()
    for h in range(KEY_VALUE_HEADS):
        for copy in arrivals(h):
            copy.start()
    metas = (meta_own, meta_near, meta_far, meta_both)
    rank = metas[0][ROWS + ROUNDS]
    count = earlier_blocks(metas, rank, KEYS)
    choose = choose_sent(scalars(mate_ref, 0, ROUNDS), scalars(metas[0], ROWS, ROUNDS))
    fill_mask(mask, (ids_own, ids_near, ids_far, ids_both), rank)
    total[...] = jnp.zeros_like(total)

    def leave(h):
        columns = part(h, 0, WIDE, WIDE)
        cargo = cargo_hbm.at[:, part(h, 0, WIDE, BUNDLE)]
        return [
            pltpu.make_async_copy(dq_ref.at[:, columns], dq_hbm.at[:, columns], left.at[0, h]),
            pltpu.make_async_copy(send_ref.at[:, columns], cargo, left.at[1, h]),
        ]

    stats_copy.wait()

    def head(h, carry):
        for copy in arrivals(h):
            copy.wait()

        for n in range(EARLIER + 1):

            @pl.when(count == n)
            def _(n=n):
                k_columns = part(h, 0, HEAD_SIZE, PAIR)
                v_columns = part(h, HEAD_SIZE, HEAD_SIZE, PAIR)
                heads = [part(h, i * HEAD_SIZE, HEAD_SIZE, WIDE) for i in range(SHARED)]
                window = pl.ds(pl.multiple_of(rank * ROWS - n * KEYS, KEYS), n * KEYS + ROWS)
                k = pairs_ref[window, k_columns]
                v = pairs_ref[window, v_columns]
                q = jnp.concatenate([q_ref[:, columns] for columns in heads], axis=0)
                g = jnp.concatenate([g_ref[:, columns] for columns in heads], axis=0)
                stats = stats_ref[h]
                logits = lax.dot_general(k, q, INNER, preferred_element_type=F32)
                allowed = jnp.concatenate([mask[window, :]] * SHARED, axis=1)
                weights = jnp.exp2(logits * EXP2_FACTOR - stats[0:1] + allowed)
                grad_weights = lax.dot_general(v, g, INNER, preferred_element_type=F32)
                grad_logits = (weights * (grad_weights - stats[1:2])).astype(BF16)
                dk = jnp.dot(grad_logits, q, preferred_element_type=F32)
                dv = jnp.dot(weights.astype(BF16), g, preferred_element_type=F32)
                total[window, k_columns] = (dk * FACTOR).astype(BF16)
                total[window, v_columns] = dv.astype(BF16)
                dq = jnp.dot(k.T, grad_logits, preferred_element_type=F32)
                dq = (dq * FACTOR).astype(BF16)
                for i, columns in enumerate(heads):
                    dq_ref[:, columns] = dq[:, i * ROWS : (i + 1) * ROWS].T

        wide = part(h, 0, WIDE, WIDE)
        send_ref[:, wide] = pick(choose, dq_ref[:, wide])
        for copy in leave(h):
            copy.start()
        return carry

    lax.fori_loop(0, KEY_VALUE_HEADS, head, 0)
    for x in range(RANKS):
        rows = total[pl.ds(pl.multiple_of((rank ^ x) * ROWS, ROWS), ROWS), :]
        pieces = pick(packing(scalars(metas[x], ROWS, ROUNDS)), rows)
        stay, turn = ((stay_keep, turn_keep), (stay_send, turn_send))[x & 1]
        stay[x >> 1] = pieces[:HALF]
        turn[x >> 1] = pieces[HALF:]
    leaving = [
        pltpu.make_async_copy(stay_keep, keep_hbm, stay_left.at[0]),
        pltpu.make_async_copy(stay_send, send_hbm, stay_left.at[1]),
    ]
    for copy in leaving:
        copy.start()
    for h in range(KEY_VALUE_HEADS):
        leaving.extend(leave(h))
    for copy in leaving:
        copy.wait()


def backward(mate, metas, q, g, pairs, stats):
    wide = (ROWS, KEY_VALUE_HEADS * WIDE)
    piece = (2, HALF, KEY_VALUE_HEADS * PAIR)
    return pl.pallas_call(
        backward_kernel,
        in_specs=[SMEM] * 5 + [VMEM] * 4 + [HBM] * 4,
        out_specs=[HBM, HBM, VMEM, VMEM, HBM, HBM],
        out_shape=[
            pltpu.HBM(wide, BF16),
            pltpu.HBM((ROWS, KEY_VALUE_HEADS * BUNDLE), BF16),
            pltpu.VMEM(piece, BF16),
            pltpu.VMEM(piece, BF16),
            pltpu.HBM(piece, BF16),
            pltpu.HBM(piece, BF16),
        ],
        scratch_shapes=[
            pltpu.VMEM(wide, BF16),
            pltpu.VMEM(wide, BF16),
            pltpu.VMEM(wide, BF16),
            pltpu.VMEM(pairs.shape, BF16),
            pltpu.VMEM(stats.shape, F32),
            pltpu.VMEM(wide, BF16),
            pltpu.VMEM(piece, BF16),
            pltpu.VMEM(piece, BF16),
            pltpu.VMEM((RANKS * ROWS, ROWS), F32),
            pltpu.VMEM(pairs.shape, BF16),
            pltpu.SemaphoreType.DMA((3, KEY_VALUE_HEADS)),
            pltpu.SemaphoreType.DMA,
            pltpu.SemaphoreType.DMA((2, KEY_VALUE_HEADS)),
            pltpu.SemaphoreType.DMA((2,)),
        ],
        compiler_params=PARAMS,
        cost_estimate=pl.CostEstimate(flops=8 * 10**9, bytes_accessed=10**7, transcendentals=4 * 10**6),
        name="backward",
    )(
        mate, *metas, *[in_vmem(meta.reshape(1, META)) for meta in metas],
        in_hbm(q), in_hbm(g), in_hbm(pairs), in_hbm(stats),
    )


def returning_kernel(mate_ref, cargo_in, own_ref, near_ref, far_ref, cargo_hbm, pairs_ref, left):
    del cargo_in
    choose = choose_sent_turns(scalars(mate_ref, 0, ROUNDS))
    leaving = []
    for h in range(KEY_VALUE_HEADS):
        columns = part(h, 0, PAIR, PAIR)
        total = (
            own_ref[0, :, columns].astype(F32) + near_ref[0, :, columns].astype(F32) + far_ref[:, columns].astype(F32)
        )
        pairs_ref[:, columns] = pick(choose, total.astype(BF16))
        cargo = cargo_hbm.at[:, part(h, WIDE, PAIR, BUNDLE)]
        leaving.append(pltpu.make_async_copy(pairs_ref.at[:, columns], cargo, left.at[h]))
        leaving[-1].start()
    for copy in leaving:
        copy.wait()


def returning(mate, cargo, own, near, far):
    return pl.pallas_call(
        returning_kernel,
        in_specs=[SMEM, HBM] + [VMEM] * 3,
        out_specs=HBM,
        out_shape=pltpu.HBM(cargo.shape, BF16),
        input_output_aliases={1: 0},
        scratch_shapes=[pltpu.VMEM((ROWS, KEY_VALUE_HEADS * PAIR), BF16), pltpu.SemaphoreType.DMA((KEY_VALUE_HEADS,))],
        compiler_params=PARAMS,
        cost_estimate=pl.CostEstimate(flops=10**8, bytes_accessed=10**6, transcendentals=0),
        name="returning",
    )(mate, in_hbm(cargo), in_vmem(own), in_vmem(near), in_vmem(far))


def merge_kernel(mate_ref, slot_ref, own_ref, landed_ref, out_ref, bring, came):
    @pl.when(pl.program_id(0) == 0)
    def _():
        bring[...] = choose_landed(scalars(mate_ref, 0, ROUNDS), scalars(slot_ref, 0, ROUNDS))
        came[...] = share_landed(bring[...])

    landed = jnp.dot(bring[...], landed_ref[...], preferred_element_type=F32)
    out_ref[...] = replaced(came[...], landed, own_ref[...])


def merge(mate, slot, own, landed):
    wide = pl.BlockSpec((ROWS, WIDE), lambda h: (0, h))
    return pl.pallas_call(
        merge_kernel,
        grid=(KEY_VALUE_HEADS,),
        in_specs=[SMEM, SMEM, wide, wide],
        out_specs=wide,
        out_shape=pltpu.HBM(own.shape, BF16),
        scratch_shapes=[pltpu.VMEM((ROWS, ROWS), BF16), pltpu.VMEM((ROWS, HEAD_SIZE), F32)],
        compiler_params=PARAMS,
        cost_estimate=pl.CostEstimate(flops=5 * 10**8, bytes_accessed=3 * 10**6, transcendentals=0),
        name="merge",
    )(mate, slot, in_hbm(own), in_vmem(landed))


def finish_kernel(
    mate_ref, slot_ref, dq_hbm, landed_ref, own_hbm, near_ref, far_ref,
    grad_q, grad_k, grad_v,
    dq_ref, own_ref, k_ref, v_ref, arrived, left,
):
    own_arriving = pltpu.make_async_copy(own_hbm, own_ref, arrived.at[1])
    own_arriving.start()
    arriving = pltpu.make_async_copy(dq_hbm, dq_ref, arrived.at[0])
    arriving.start()
    mate, slot = scalars(mate_ref, 0, ROUNDS), scalars(slot_ref, 0, ROUNDS)
    bring = choose_landed(mate, slot)
    came = share_landed(bring)
    place = unpacking(slot)[:, :HALF]
    own_arriving.wait()
    for h in range(KEY_VALUE_HEADS):
        columns = part(h, 0, PAIR, PAIR)
        total = (
            own_ref[0, :, columns].astype(F32) + near_ref[0, :, columns].astype(F32) + far_ref[:, columns].astype(F32)
        )
        landed = jnp.dot(bring, landed_ref[:, part(h, WIDE, PAIR, BUNDLE)], preferred_element_type=F32)
        pairs = (jnp.dot(place, total.astype(BF16), preferred_element_type=F32) + landed).astype(BF16)
        k_ref[:, part(h, 0, HEAD_SIZE, HEAD_SIZE)] = pairs[:, :HEAD_SIZE]
        v_ref[:, part(h, 0, HEAD_SIZE, HEAD_SIZE)] = pairs[:, HEAD_SIZE:]
    leaving = [
        pltpu.make_async_copy(k_ref, grad_k, left.at[0]),
        pltpu.make_async_copy(v_ref, grad_v, left.at[1]),
    ]
    for copy in leaving:
        copy.start()
    arriving.wait()
    for h in range(KEY_VALUE_HEADS):
        columns = part(h, 0, WIDE, WIDE)
        landed = jnp.dot(bring, landed_ref[:, part(h, 0, WIDE, BUNDLE)], preferred_element_type=F32)
        dq_ref[:, columns] = replaced(came, landed, dq_ref[:, columns])
        copy = pltpu.make_async_copy(dq_ref.at[:, columns], grad_q.at[:, columns], left.at[2 + h])
        copy.start()
        leaving.append(copy)
    for copy in leaving:
        copy.wait()


def finish(mate, slot, dq, landed, own, near, far):
    narrow = (ROWS, KEY_VALUE_HEADS * HEAD_SIZE)
    return pl.pallas_call(
        finish_kernel,
        in_specs=[SMEM, SMEM, HBM, VMEM, HBM, VMEM, VMEM],
        out_specs=[HBM] * 3,
        out_shape=[pltpu.HBM(dq.shape, BF16), pltpu.HBM(narrow, BF16), pltpu.HBM(narrow, BF16)],
        scratch_shapes=[
            pltpu.VMEM(dq.shape, BF16),
            pltpu.VMEM(own.shape, BF16),
            pltpu.VMEM(narrow, BF16),
            pltpu.VMEM(narrow, BF16),
            pltpu.SemaphoreType.DMA((2,)),
            pltpu.SemaphoreType.DMA((2 + KEY_VALUE_HEADS,)),
        ],
        compiler_params=PARAMS,
        cost_estimate=pl.CostEstimate(flops=8 * 10**8, bytes_accessed=5 * 10**6, transcendentals=0),
        name="finish",
    )(mate, slot, in_hbm(dq), in_vmem(landed), in_hbm(own), in_vmem(near), in_vmem(far))


def exchange(rows):
    blocks = rows.reshape(GROUPS, BLOCK, rows.shape[-1])
    return lax.all_to_all(blocks, "dp", split_axis=0, concat_axis=0, tiled=True).reshape(rows.shape)


def across(array):
    return lax.ppermute(array, "sp", [(i, i ^ 2) for i in range(RANKS)])


def beside(array):
    return lax.ppermute(array, "sp", [(i, i ^ 1) for i in range(RANKS)])


def spread(array):
    far = across(array)
    return array, beside(array), far, beside(far)


def partial_sum(keep, near):
    return (keep[1].astype(F32) + near[1].astype(F32)).astype(BF16)


def body(queries, keys, values, cotangent, doc_ids, partners, swap_slots):
    q, k, v, g = queries[0], keys[0], values[0], cotangent[0]
    mate = in_hbm(partners.reshape(ROUNDS))
    slots = swap_slots.reshape(ROUNDS)
    slot = in_hbm(slots)
    rank = lax.axis_index("sp").astype(jnp.int32).reshape(1)
    meta = jnp.concatenate(
        [doc_ids.reshape(ROWS), slots, rank, jnp.zeros((META - ROWS - ROUNDS - 1,), jnp.int32)]
    )

    stay = staying(slot, k, v)
    stay_far = across(stay)
    send = outgoing(mate, slot, q, k, v, g)
    send, stay_far = lax.optimization_barrier((send, stay_far))
    landed = exchange(send)
    stays = stay, beside(stay), stay_far, beside(stay_far)
    metas = meta, beside(meta), across(meta), lax.ppermute(meta, "sp", [(i, i ^ 3) for i in range(RANKS)])
    landed, stays, metas = lax.optimization_barrier((landed, stays, metas))
    turns = spread(traded_pairs(mate, landed))
    out, send, *kept = forward(mate, metas, q, g, landed, stays, turns)
    landed_out = exchange(send)
    dq, send, turn_keep, turn_send, stay_keep, stay_send = backward(mate, metas, *kept)
    turn_near, stay_near = beside(turn_send), beside(stay_send)
    partials = partial_sum(turn_keep, turn_near), partial_sum(stay_keep, stay_near)
    landed_out, partials = lax.optimization_barrier((landed_out, partials))
    turn_far, stay_far = across(partials[0]), across(partials[1])
    send = returning(mate, send, turn_keep, turn_near, turn_far)
    send, stay_far = lax.optimization_barrier((send, stay_far))
    landed = exchange(send)
    attended = merge(mate, slot, out, landed_out)
    grad_q, grad_k, grad_v = finish(mate, slot, dq, landed, stay_keep, stay_near, stay_far)
    return attended[None], grad_q[None], grad_k[None], grad_v[None]


def solution(mesh):
    rows = P("dp", "sp", None)
    return jax.shard_map(
        body,
        mesh=mesh,
        in_specs=(rows, rows, rows, rows, P("dp", "sp"), P(None, "dp"), rows),
        out_specs=(rows, rows, rows, rows),
        check_vma=False,
    )
```

```python
import jax
import jax.numpy as jnp
from jax import lax
from jax.experimental import pallas as pl
from jax.experimental.pallas import tpu as pltpu
from jax.sharding import PartitionSpec as P

KEY_VALUE_HEADS = 4
SHARED = 4
HEAD_SIZE = 128
BLOCK = 8
ROUNDS = 16
ROWS = 256
HALF = ROUNDS * BLOCK
GROUPS = 32
RANKS = 4
WIDE = SHARED * HEAD_SIZE
PAIR = 2 * HEAD_SIZE
BUNDLE = WIDE + PAIR
CARGO = 2 * WIDE + PAIR
META = 384
KEYS = 128
TOGETHER = 2
EARLIER = (RANKS - 1) * ROWS // KEYS
FACTOR = HEAD_SIZE ** (-0.5)
EXP2_FACTOR = FACTOR * 1.4426950408889634
MASKED = -1e30
BF16 = jnp.bfloat16
F32 = jnp.float32

SMEM = pl.BlockSpec(memory_space=pltpu.SMEM)
VMEM = pl.BlockSpec(memory_space=pltpu.VMEM)
HBM = pl.BlockSpec(memory_space=pl.ANY)
PARAMS = pltpu.CompilerParams(vmem_limit_bytes=28 * 1024 * 1024)


def in_hbm(array):
    return pltpu.with_memory_space_constraint(array, pltpu.HBM)


def in_vmem(array):
    return pltpu.with_memory_space_constraint(array, pltpu.VMEM)


def iota(shape, axis):
    return lax.broadcasted_iota(jnp.int32, shape, axis)


def onehot(hit):
    return jnp.where(hit, 1.0, 0.0).astype(BF16)


def pick(matrix, rows):
    return jnp.dot(matrix, rows, preferred_element_type=F32).astype(BF16)


def part(h, first, width, whole):
    return pl.ds(pl.multiple_of(h * whole + first, HEAD_SIZE), width)


def lanes(width):
    return iota((1, width), 1)


def matching(value, keys, results):
    found = jnp.full_like(value, -1)
    for key, result in zip(keys, results):
        found = jnp.where(value == key, result, found)
    return found


def rows_at(block, place):
    return jnp.where(block >= 0, block * BLOCK + (place & 7), -1)


def placing(target, count):
    return onehot(target == iota((count, target.shape[1]), 0))


def choose_sent(mate, slot):
    place = lanes(ROWS)
    return placing(rows_at(matching(place >> 3, slot, mate), place), ROWS)


def choose_landed(mate, slot):
    place = lanes(ROWS)
    return placing(rows_at(matching(place >> 3, mate, slot), place), ROWS)


def choose_turns(mate):
    place = lanes(ROWS)
    return placing(rows_at(matching(place >> 3, mate, range(ROUNDS)), place), HALF)


def choose_sent_turns(mate):
    place = lanes(HALF)
    return placing(rows_at(matching(place >> 3, range(ROUNDS), mate), place), ROWS)


def packed_row(slot):
    place = lanes(ROWS)
    block = place >> 3
    turn = matching(block, slot, range(ROUNDS))
    lower = jnp.zeros_like(place)
    for t in range(ROUNDS):
        lower = lower + jnp.where(block > slot[t], 1, 0)
    return jnp.where(turn >= 0, HALF + turn * BLOCK, (block - lower) * BLOCK) + (place & 7)


def packing(slot, count=ROWS):
    return placing(packed_row(slot), count)


def unpacking(slot):
    hit = jnp.where(packed_row(slot) == iota((ROWS, ROWS), 0), 1.0, 0.0)
    return hit.T.astype(BF16)


def share_landed(matrix):
    return jnp.broadcast_to(jnp.sum(matrix.astype(F32), axis=1, keepdims=True), (ROWS, HEAD_SIZE))


def replaced(came, landed, own):
    mask = jnp.concatenate([came] * (own.shape[1] // HEAD_SIZE), axis=1)
    return jnp.where(mask > 0.5, landed, own.astype(F32)).astype(BF16)


def scalars(ref, first, count):
    return [ref[first + t] for t in range(count)]


def staying_kernel(slot_ref, k_hbm, v_hbm, stay_ref, k_ref, v_ref, arrived):
    copies = [pltpu.make_async_copy(k_hbm, k_ref, arrived.at[0]), pltpu.make_async_copy(v_hbm, v_ref, arrived.at[1])]
    for copy in copies:
        copy.start()
    keep = packing(scalars(slot_ref, 0, ROUNDS), HALF)
    for copy in copies:
        copy.wait()
    for h in range(KEY_VALUE_HEADS):
        head = part(h, 0, HEAD_SIZE, HEAD_SIZE)
        stay_ref[:, part(h, 0, PAIR, PAIR)] = pick(keep, jnp.concatenate([k_ref[:, head], v_ref[:, head]], axis=1))


def staying(slot, k, v):
    return pl.pallas_call(
        staying_kernel,
        in_specs=[SMEM, HBM, HBM],
        out_specs=VMEM,
        out_shape=pltpu.VMEM((HALF, KEY_VALUE_HEADS * PAIR), BF16),
        scratch_shapes=[pltpu.VMEM(k.shape, BF16), pltpu.VMEM(v.shape, BF16), pltpu.SemaphoreType.DMA((2,))],
        compiler_params=PARAMS,
        cost_estimate=pl.CostEstimate(flops=10**8, bytes_accessed=10**6, transcendentals=0),
        name="staying",
    )(slot, in_hbm(k), in_hbm(v))


def outgoing_kernel(mate_ref, slot_ref, q_ref, k_ref, v_ref, g_ref, send_ref, choose):
    @pl.when(pl.program_id(0) == 0)
    def _():
        choose[...] = choose_sent(scalars(mate_ref, 0, ROUNDS), scalars(slot_ref, 0, ROUNDS))

    rows = jnp.concatenate([q_ref[...], k_ref[...], v_ref[...], g_ref[...]], axis=1)
    send_ref[...] = pick(choose[...], rows)


def outgoing(mate, slot, q, k, v, g):
    wide = pl.BlockSpec((ROWS, WIDE), lambda h: (0, h))
    head = pl.BlockSpec((ROWS, HEAD_SIZE), lambda h: (0, h))
    return pl.pallas_call(
        outgoing_kernel,
        grid=(KEY_VALUE_HEADS,),
        in_specs=[SMEM, SMEM, wide, head, head, wide],
        out_specs=pl.BlockSpec((ROWS, CARGO), lambda h: (0, h)),
        out_shape=pltpu.HBM((ROWS, KEY_VALUE_HEADS * CARGO), BF16),
        scratch_shapes=[pltpu.VMEM((ROWS, ROWS), BF16)],
        compiler_params=PARAMS,
        cost_estimate=pl.CostEstimate(flops=10**9, bytes_accessed=5 * 10**6, transcendentals=0),
        name="outgoing",
    )(mate, slot, in_hbm(q), in_hbm(k), in_hbm(v), in_hbm(g))


def traded_pairs_kernel(mate_ref, landed_ref, out_ref):
    choose = choose_turns(scalars(mate_ref, 0, ROUNDS))
    for h in range(KEY_VALUE_HEADS):
        out_ref[:, part(h, 0, PAIR, PAIR)] = pick(choose, landed_ref[:, part(h, WIDE, PAIR, CARGO)])


def traded_pairs(mate, landed):
    return pl.pallas_call(
        traded_pairs_kernel,
        in_specs=[SMEM, VMEM],
        out_specs=VMEM,
        out_shape=pltpu.VMEM((HALF, KEY_VALUE_HEADS * PAIR), BF16),
        compiler_params=PARAMS,
        cost_estimate=pl.CostEstimate(flops=10**8, bytes_accessed=8 * 10**5, transcendentals=0),
        name="traded_pairs",
    )(mate, in_vmem(landed))


def to_column(row):
    here = iota((ROWS, ROWS), 0) == iota((ROWS, ROWS), 1)
    return jnp.sum(jnp.where(here, row, 0.0), axis=1, keepdims=True)


def earlier_blocks(metas, rank, keys):
    first = metas[0][0]
    count = jnp.int32(0)
    for x in (1, 2, 3):
        for last in range(keys - 1, ROWS, keys):
            count = count + jnp.where(((rank ^ x) < rank) & (metas[x][last] == first), 1, 0)
    return count


def fill_mask(mask, metas_ids, rank, reach):
    ids = [piece[:, :ROWS].astype(F32) for piece in metas_ids]
    for x in range(RANKS):
        other = rank ^ x

        @pl.when((other <= rank) & ((rank - other - 1) * ROWS < reach))
        def _(x=x, other=other):
            allowed = to_column(ids[x]) == ids[0]
            if x == 0:
                allowed = allowed & (iota((ROWS, 1), 0) <= lanes(ROWS))
            mask[pl.ds(pl.multiple_of(other * ROWS, ROWS), ROWS), :] = jnp.where(allowed, 0.0, MASKED)


INNER = (((1,), (1,)), ((), ()))


def forward_kernel(
    mate_ref, meta_own, meta_near, meta_far, meta_both, ids_own, ids_near, ids_far, ids_both,
    q_hbm, g_hbm, landed_ref, stay_own, stay_near, stay_far, stay_both, turn_own, turn_near, turn_far, turn_both,
    out_hbm, send_hbm, q_kept, g_kept, pairs_kept, stats_hbm,
    out_ref, send_ref, q_ref, g_ref, pairs_ref, stats_ref, bring, place, mask, came, q_arrived, g_arrived, left,
):
    q_copy = pltpu.make_async_copy(q_hbm, q_ref, q_arrived)
    g_copy = pltpu.make_async_copy(g_hbm, g_ref, g_arrived)
    q_copy.start()
    g_copy.start()
    metas = (meta_own, meta_near, meta_far, meta_both)
    rank = metas[0][ROWS + ROUNDS]
    count = earlier_blocks(metas, rank, ROWS)
    mate, slot = scalars(mate_ref, 0, ROUNDS), scalars(metas[0], ROWS, ROUNDS)
    choose = choose_sent(mate, slot)
    bring[...] = choose_landed(mate, slot)
    came[...] = share_landed(bring[...])
    fill_mask(mask, (ids_own, ids_near, ids_far, ids_both), rank, count * ROWS)
    stay = (stay_own, stay_near, stay_far, stay_both)
    turn = (turn_own, turn_near, turn_far, turn_both)
    for x in range(RANKS):
        other = rank ^ x

        @pl.when((other <= rank) & (rank - other <= count))
        def _(x=x, other=other):
            rows = jnp.concatenate([stay[x][...], turn[x][...]], axis=0)
            place[...] = unpacking(scalars(metas[x], ROWS, ROUNDS))
            pairs_ref[pl.ds(pl.multiple_of(other * ROWS, ROWS), ROWS), :] = pick(place[...], rows)

    q_copy.wait()
    g_copy.wait()

    def leave(h, turn, source, target, whole):
        columns = part(h, 0, whole, whole)
        return pltpu.make_async_copy(source.at[:, columns], target.at[:, columns], left.at[turn, h])

    def leave_early(h):
        return [leave(h, 0, q_ref, q_kept, WIDE), leave(h, 1, g_ref, g_kept, WIDE), leave(h, 2, pairs_ref, pairs_kept, PAIR)]

    def leave_late(h):
        return [leave(h, 3, out_ref, out_hbm, WIDE), leave(h, 4, send_ref, send_hbm, WIDE)]

    def merged(h):
        wide = part(h, 0, WIDE, WIDE)
        came_q = jnp.dot(bring[...], landed_ref[:, part(h, 0, WIDE, CARGO)], preferred_element_type=F32)
        came_g = jnp.dot(bring[...], landed_ref[:, part(h, BUNDLE, WIDE, CARGO)], preferred_element_type=F32)
        q_ref[:, wide] = replaced(came[...], came_q, q_ref[:, wide])
        g_ref[:, wide] = replaced(came[...], came_g, g_ref[:, wide])
        for copy in leave_early(h):
            copy.start()

    def attend(h, n):
        window = pl.ds(pl.multiple_of(rank * ROWS - n * ROWS, ROWS), n * ROWS + ROWS)
        k = pairs_ref[window, part(h, 0, HEAD_SIZE, PAIR)]
        v_turned = pairs_ref[window, part(h, HEAD_SIZE, HEAD_SIZE, PAIR)].T
        heads = [part(h, i * HEAD_SIZE, HEAD_SIZE, WIDE) for i in range(SHARED)]
        q = jnp.concatenate([q_ref[:, columns] for columns in heads], axis=0)
        g_turned = jnp.concatenate([g_ref[:, columns].T for columns in heads], axis=1)
        logits = lax.dot_general(k, q, INNER, preferred_element_type=F32)
        logits = logits + jnp.concatenate([mask[window, :]] * SHARED, axis=1)
        top = jnp.max(logits, axis=0, keepdims=True)
        raised = jnp.exp2((logits - top) * EXP2_FACTOR)
        total = jnp.sum(raised, axis=0, keepdims=True)
        out = jnp.dot(v_turned, raised.astype(BF16), preferred_element_type=F32) * (1.0 / total)
        inner = jnp.sum(out * g_turned.astype(F32), axis=0, keepdims=True)
        out = out.astype(BF16)
        for i, columns in enumerate(heads):
            out_ref[:, columns] = out[:, i * ROWS : (i + 1) * ROWS].T
        stats_ref[h] = jnp.concatenate([top * EXP2_FACTOR + jnp.log2(total), inner], axis=0)

    def sent(h):
        wide = part(h, 0, WIDE, WIDE)
        send_ref[:, wide] = pick(choose, out_ref[:, wide])
        for copy in leave_late(h):
            copy.start()

    def heads_at(step, carry):
        heads = [step * TOGETHER + i for i in range(TOGETHER)]
        for h in heads:
            merged(h)
        for n in range(RANKS):

            @pl.when(count == n)
            def _(n=n):
                for h in heads:
                    attend(h, n)

        for h in heads:
            sent(h)
        return carry

    lax.fori_loop(0, KEY_VALUE_HEADS // TOGETHER, heads_at, 0)
    stats_copy = pltpu.make_async_copy(stats_ref, stats_hbm, q_arrived)
    stats_copy.start()
    for h in range(KEY_VALUE_HEADS):
        for copy in leave_early(h) + leave_late(h):
            copy.wait()
    stats_copy.wait()


def forward(mate, metas, q, g, landed, stays, turns):
    wide = (ROWS, KEY_VALUE_HEADS * WIDE)
    return pl.pallas_call(
        forward_kernel,
        in_specs=[SMEM] * 5 + [VMEM] * 4 + [HBM] * 2 + [VMEM] * (1 + 2 * RANKS),
        out_specs=[HBM] * 6,
        out_shape=[
            pltpu.HBM(wide, BF16),
            pltpu.HBM(wide, BF16),
            pltpu.HBM(wide, BF16),
            pltpu.HBM(wide, BF16),
            pltpu.HBM((RANKS * ROWS, KEY_VALUE_HEADS * PAIR), BF16),
            pltpu.HBM((KEY_VALUE_HEADS, 2, SHARED * ROWS), F32),
        ],
        scratch_shapes=[
            pltpu.VMEM(wide, BF16),
            pltpu.VMEM(wide, BF16),
            pltpu.VMEM(wide, BF16),
            pltpu.VMEM(wide, BF16),
            pltpu.VMEM((RANKS * ROWS, KEY_VALUE_HEADS * PAIR), BF16),
            pltpu.VMEM((KEY_VALUE_HEADS, 2, SHARED * ROWS), F32),
            pltpu.VMEM((ROWS, ROWS), BF16),
            pltpu.VMEM((ROWS, ROWS), BF16),
            pltpu.VMEM((RANKS * ROWS, ROWS), F32),
            pltpu.VMEM((ROWS, HEAD_SIZE), F32),
            pltpu.SemaphoreType.DMA,
            pltpu.SemaphoreType.DMA,
            pltpu.SemaphoreType.DMA((5, KEY_VALUE_HEADS)),
        ],
        compiler_params=PARAMS,
        cost_estimate=pl.CostEstimate(flops=4 * 10**9, bytes_accessed=10**7, transcendentals=4 * 10**6),
        name="forward",
    )(
        mate, *metas, *[in_vmem(meta.reshape(1, META)) for meta in metas],
        in_hbm(q), in_hbm(g), in_vmem(landed), *[in_vmem(x) for x in (*stays, *turns)],
    )


def backward_kernel(
    mate_ref, meta_own, meta_near, meta_far, meta_both, ids_own, ids_near, ids_far, ids_both,
    q_hbm, g_hbm, pairs_hbm, stats_hbm,
    dq_hbm, cargo_hbm, turn_keep, turn_send, keep_hbm, send_hbm,
    send_ref, q_ref, g_ref, pairs_ref, stats_ref, dq_ref, stay_keep, stay_send, mask, total, arrived, stats_arrived, left, stay_left,
):
    def arrive(h, turn, source, target, whole):
        columns = part(h, 0, whole, whole)
        return pltpu.make_async_copy(source.at[:, columns], target.at[:, columns], arrived.at[turn, h])

    def arrivals(h):
        return [arrive(h, 0, pairs_hbm, pairs_ref, PAIR), arrive(h, 1, q_hbm, q_ref, WIDE), arrive(h, 2, g_hbm, g_ref, WIDE)]

    stats_copy = pltpu.make_async_copy(stats_hbm, stats_ref, stats_arrived)
    stats_copy.start()
    for h in range(KEY_VALUE_HEADS):
        for copy in arrivals(h):
            copy.start()
    metas = (meta_own, meta_near, meta_far, meta_both)
    rank = metas[0][ROWS + ROUNDS]
    count = earlier_blocks(metas, rank, KEYS)
    choose = choose_sent(scalars(mate_ref, 0, ROUNDS), scalars(metas[0], ROWS, ROUNDS))
    fill_mask(mask, (ids_own, ids_near, ids_far, ids_both), rank, count * KEYS)
    total[...] = jnp.zeros_like(total)

    def leave(h):
        columns = part(h, 0, WIDE, WIDE)
        cargo = cargo_hbm.at[:, part(h, 0, WIDE, BUNDLE)]
        return [
            pltpu.make_async_copy(dq_ref.at[:, columns], dq_hbm.at[:, columns], left.at[0, h]),
            pltpu.make_async_copy(send_ref.at[:, columns], cargo, left.at[1, h]),
        ]

    stats_copy.wait()

    def head(h, carry):
        for copy in arrivals(h):
            copy.wait()

        for n in range(EARLIER + 1):

            @pl.when(count == n)
            def _(n=n):
                k_columns = part(h, 0, HEAD_SIZE, PAIR)
                v_columns = part(h, HEAD_SIZE, HEAD_SIZE, PAIR)
                heads = [part(h, i * HEAD_SIZE, HEAD_SIZE, WIDE) for i in range(SHARED)]
                window = pl.ds(pl.multiple_of(rank * ROWS - n * KEYS, KEYS), n * KEYS + ROWS)
                k = pairs_ref[window, k_columns]
                v = pairs_ref[window, v_columns]
                q = jnp.concatenate([q_ref[:, columns] for columns in heads], axis=0)
                g = jnp.concatenate([g_ref[:, columns] for columns in heads], axis=0)
                stats = stats_ref[h]
                logits = lax.dot_general(k, q, INNER, preferred_element_type=F32)
                allowed = jnp.concatenate([mask[window, :]] * SHARED, axis=1)
                weights = jnp.exp2(logits * EXP2_FACTOR - stats[0:1] + allowed)
                grad_weights = lax.dot_general(v, g, INNER, preferred_element_type=F32)
                grad_logits = (weights * (grad_weights - stats[1:2])).astype(BF16)
                dk = jnp.dot(grad_logits, q, preferred_element_type=F32)
                dv = jnp.dot(weights.astype(BF16), g, preferred_element_type=F32)
                total[window, k_columns] = (dk * FACTOR).astype(BF16)
                total[window, v_columns] = dv.astype(BF16)
                dq = jnp.dot(k.T, grad_logits, preferred_element_type=F32)
                dq = (dq * FACTOR).astype(BF16)
                for i, columns in enumerate(heads):
                    dq_ref[:, columns] = dq[:, i * ROWS : (i + 1) * ROWS].T

        wide = part(h, 0, WIDE, WIDE)
        send_ref[:, wide] = pick(choose, dq_ref[:, wide])
        for copy in leave(h):
            copy.start()
        return carry

    lax.fori_loop(0, KEY_VALUE_HEADS, head, 0)
    for x in range(RANKS):
        other = rank ^ x
        stay, turn = ((stay_keep, turn_keep), (stay_send, turn_send))[x & 1]
        reached = (other <= rank) & ((rank - other - 1) * ROWS < count * KEYS)

        @pl.when(reached)
        def _(x=x, other=other, stay=stay, turn=turn):
            rows = total[pl.ds(pl.multiple_of(other * ROWS, ROWS), ROWS), :]
            pieces = pick(packing(scalars(metas[x], ROWS, ROUNDS)), rows)
            stay[x >> 1] = pieces[:HALF]
            turn[x >> 1] = pieces[HALF:]

        @pl.when(jnp.logical_not(reached))
        def _(x=x, stay=stay, turn=turn):
            stay[x >> 1] = jnp.zeros(stay.shape[1:], BF16)
            turn[x >> 1] = jnp.zeros(turn.shape[1:], BF16)

    leaving = [
        pltpu.make_async_copy(stay_keep, keep_hbm, stay_left.at[0]),
        pltpu.make_async_copy(stay_send, send_hbm, stay_left.at[1]),
    ]
    for copy in leaving:
        copy.start()
    for h in range(KEY_VALUE_HEADS):
        leaving.extend(leave(h))
    for copy in leaving:
        copy.wait()


def backward(mate, metas, q, g, pairs, stats):
    wide = (ROWS, KEY_VALUE_HEADS * WIDE)
    piece = (2, HALF, KEY_VALUE_HEADS * PAIR)
    return pl.pallas_call(
        backward_kernel,
        in_specs=[SMEM] * 5 + [VMEM] * 4 + [HBM] * 4,
        out_specs=[HBM, HBM, VMEM, VMEM, HBM, HBM],
        out_shape=[
            pltpu.HBM(wide, BF16),
            pltpu.HBM((ROWS, KEY_VALUE_HEADS * BUNDLE), BF16),
            pltpu.VMEM(piece, BF16),
            pltpu.VMEM(piece, BF16),
            pltpu.HBM(piece, BF16),
            pltpu.HBM(piece, BF16),
        ],
        scratch_shapes=[
            pltpu.VMEM(wide, BF16),
            pltpu.VMEM(wide, BF16),
            pltpu.VMEM(wide, BF16),
            pltpu.VMEM(pairs.shape, BF16),
            pltpu.VMEM(stats.shape, F32),
            pltpu.VMEM(wide, BF16),
            pltpu.VMEM(piece, BF16),
            pltpu.VMEM(piece, BF16),
            pltpu.VMEM((RANKS * ROWS, ROWS), F32),
            pltpu.VMEM(pairs.shape, BF16),
            pltpu.SemaphoreType.DMA((3, KEY_VALUE_HEADS)),
            pltpu.SemaphoreType.DMA,
            pltpu.SemaphoreType.DMA((2, KEY_VALUE_HEADS)),
            pltpu.SemaphoreType.DMA((2,)),
        ],
        compiler_params=PARAMS,
        cost_estimate=pl.CostEstimate(flops=8 * 10**9, bytes_accessed=10**7, transcendentals=4 * 10**6),
        name="backward",
    )(
        mate, *metas, *[in_vmem(meta.reshape(1, META)) for meta in metas],
        in_hbm(q), in_hbm(g), in_hbm(pairs), in_hbm(stats),
    )


def returning_kernel(mate_ref, cargo_in, own_ref, near_ref, far_ref, cargo_hbm, pairs_ref, left):
    del cargo_in
    choose = choose_sent_turns(scalars(mate_ref, 0, ROUNDS))
    leaving = []
    for h in range(KEY_VALUE_HEADS):
        columns = part(h, 0, PAIR, PAIR)
        total = (
            own_ref[0, :, columns].astype(F32) + near_ref[0, :, columns].astype(F32) + far_ref[:, columns].astype(F32)
        )
        pairs_ref[:, columns] = pick(choose, total.astype(BF16))
        cargo = cargo_hbm.at[:, part(h, WIDE, PAIR, BUNDLE)]
        leaving.append(pltpu.make_async_copy(pairs_ref.at[:, columns], cargo, left.at[h]))
        leaving[-1].start()
    for copy in leaving:
        copy.wait()


def returning(mate, cargo, own, near, far):
    return pl.pallas_call(
        returning_kernel,
        in_specs=[SMEM, HBM] + [VMEM] * 3,
        out_specs=HBM,
        out_shape=pltpu.HBM(cargo.shape, BF16),
        input_output_aliases={1: 0},
        scratch_shapes=[pltpu.VMEM((ROWS, KEY_VALUE_HEADS * PAIR), BF16), pltpu.SemaphoreType.DMA((KEY_VALUE_HEADS,))],
        compiler_params=PARAMS,
        cost_estimate=pl.CostEstimate(flops=10**8, bytes_accessed=10**6, transcendentals=0),
        name="returning",
    )(mate, in_hbm(cargo), in_vmem(own), in_vmem(near), in_vmem(far))


def merge_kernel(mate_ref, slot_ref, own_ref, landed_ref, out_ref, bring, came):
    @pl.when(pl.program_id(0) == 0)
    def _():
        bring[...] = choose_landed(scalars(mate_ref, 0, ROUNDS), scalars(slot_ref, 0, ROUNDS))
        came[...] = share_landed(bring[...])

    landed = jnp.dot(bring[...], landed_ref[...], preferred_element_type=F32)
    out_ref[...] = replaced(came[...], landed, own_ref[...])


def merge(mate, slot, own, landed):
    wide = pl.BlockSpec((ROWS, WIDE), lambda h: (0, h))
    return pl.pallas_call(
        merge_kernel,
        grid=(KEY_VALUE_HEADS,),
        in_specs=[SMEM, SMEM, wide, wide],
        out_specs=wide,
        out_shape=pltpu.HBM(own.shape, BF16),
        scratch_shapes=[pltpu.VMEM((ROWS, ROWS), BF16), pltpu.VMEM((ROWS, HEAD_SIZE), F32)],
        compiler_params=PARAMS,
        cost_estimate=pl.CostEstimate(flops=5 * 10**8, bytes_accessed=3 * 10**6, transcendentals=0),
        name="merge",
    )(mate, slot, in_hbm(own), in_vmem(landed))


def finish_kernel(
    mate_ref, slot_ref, dq_hbm, landed_ref, own_hbm, near_ref, far_ref,
    grad_q, grad_k, grad_v,
    dq_ref, own_ref, k_ref, v_ref, arrived, left,
):
    own_arriving = pltpu.make_async_copy(own_hbm, own_ref, arrived.at[1])
    own_arriving.start()
    arriving = pltpu.make_async_copy(dq_hbm, dq_ref, arrived.at[0])
    arriving.start()
    mate, slot = scalars(mate_ref, 0, ROUNDS), scalars(slot_ref, 0, ROUNDS)
    bring = choose_landed(mate, slot)
    came = share_landed(bring)
    place = unpacking(slot)[:, :HALF]
    own_arriving.wait()
    for h in range(KEY_VALUE_HEADS):
        columns = part(h, 0, PAIR, PAIR)
        total = (
            own_ref[0, :, columns].astype(F32) + near_ref[0, :, columns].astype(F32) + far_ref[:, columns].astype(F32)
        )
        landed = jnp.dot(bring, landed_ref[:, part(h, WIDE, PAIR, BUNDLE)], preferred_element_type=F32)
        pairs = (jnp.dot(place, total.astype(BF16), preferred_element_type=F32) + landed).astype(BF16)
        k_ref[:, part(h, 0, HEAD_SIZE, HEAD_SIZE)] = pairs[:, :HEAD_SIZE]
        v_ref[:, part(h, 0, HEAD_SIZE, HEAD_SIZE)] = pairs[:, HEAD_SIZE:]
    leaving = [
        pltpu.make_async_copy(k_ref, grad_k, left.at[0]),
        pltpu.make_async_copy(v_ref, grad_v, left.at[1]),
    ]
    for copy in leaving:
        copy.start()
    arriving.wait()
    for h in range(KEY_VALUE_HEADS):
        columns = part(h, 0, WIDE, WIDE)
        landed = jnp.dot(bring, landed_ref[:, part(h, 0, WIDE, BUNDLE)], preferred_element_type=F32)
        dq_ref[:, columns] = replaced(came, landed, dq_ref[:, columns])
        copy = pltpu.make_async_copy(dq_ref.at[:, columns], grad_q.at[:, columns], left.at[2 + h])
        copy.start()
        leaving.append(copy)
    for copy in leaving:
        copy.wait()


def finish(mate, slot, dq, landed, own, near, far):
    narrow = (ROWS, KEY_VALUE_HEADS * HEAD_SIZE)
    return pl.pallas_call(
        finish_kernel,
        in_specs=[SMEM, SMEM, HBM, VMEM, HBM, VMEM, VMEM],
        out_specs=[HBM] * 3,
        out_shape=[pltpu.HBM(dq.shape, BF16), pltpu.HBM(narrow, BF16), pltpu.HBM(narrow, BF16)],
        scratch_shapes=[
            pltpu.VMEM(dq.shape, BF16),
            pltpu.VMEM(own.shape, BF16),
            pltpu.VMEM(narrow, BF16),
            pltpu.VMEM(narrow, BF16),
            pltpu.SemaphoreType.DMA((2,)),
            pltpu.SemaphoreType.DMA((2 + KEY_VALUE_HEADS,)),
        ],
        compiler_params=PARAMS,
        cost_estimate=pl.CostEstimate(flops=8 * 10**8, bytes_accessed=5 * 10**6, transcendentals=0),
        name="finish",
    )(mate, slot, in_hbm(dq), in_vmem(landed), in_hbm(own), in_vmem(near), in_vmem(far))


def exchange(rows):
    blocks = rows.reshape(GROUPS, BLOCK, rows.shape[-1])
    return lax.all_to_all(blocks, "dp", split_axis=0, concat_axis=0, tiled=True).reshape(rows.shape)


def across(array):
    return lax.ppermute(array, "sp", [(i, i ^ 2) for i in range(RANKS)])


def beside(array):
    return lax.ppermute(array, "sp", [(i, i ^ 1) for i in range(RANKS)])


def spread(array):
    far = across(array)
    return array, beside(array), far, beside(far)


def partial_sum(keep, near):
    return (keep[1].astype(F32) + near[1].astype(F32)).astype(BF16)


def body(queries, keys, values, cotangent, doc_ids, partners, swap_slots):
    q, k, v, g = queries[0], keys[0], values[0], cotangent[0]
    mate = in_hbm(partners.reshape(ROUNDS))
    slots = swap_slots.reshape(ROUNDS)
    slot = in_hbm(slots)
    rank = lax.axis_index("sp").astype(jnp.int32).reshape(1)
    meta = jnp.concatenate(
        [doc_ids.reshape(ROWS), slots, rank, jnp.zeros((META - ROWS - ROUNDS - 1,), jnp.int32)]
    )

    stay = staying(slot, k, v)
    stay_far = across(stay)
    send = outgoing(mate, slot, q, k, v, g)
    send, stay_far = lax.optimization_barrier((send, stay_far))
    landed = exchange(send)
    stays = stay, beside(stay), stay_far, beside(stay_far)
    metas = meta, beside(meta), across(meta), lax.ppermute(meta, "sp", [(i, i ^ 3) for i in range(RANKS)])
    landed, stays, metas = lax.optimization_barrier((landed, stays, metas))
    turns = spread(traded_pairs(mate, landed))
    out, send, *kept = forward(mate, metas, q, g, landed, stays, turns)
    landed_out = exchange(send)
    dq, send, turn_keep, turn_send, stay_keep, stay_send = backward(mate, metas, *kept)
    turn_near, stay_near = beside(turn_send), beside(stay_send)
    partials = partial_sum(turn_keep, turn_near), partial_sum(stay_keep, stay_near)
    landed_out, partials = lax.optimization_barrier((landed_out, partials))
    turn_far, stay_far = across(partials[0]), across(partials[1])
    send = returning(mate, send, turn_keep, turn_near, turn_far)
    send, stay_far = lax.optimization_barrier((send, stay_far))
    landed = exchange(send)
    attended = merge(mate, slot, out, landed_out)
    grad_q, grad_k, grad_v = finish(mate, slot, dq, landed, stay_keep, stay_near, stay_far)
    return attended[None], grad_q[None], grad_k[None], grad_v[None]


def solution(mesh):
    rows = P("dp", "sp", None)
    return jax.shard_map(
        body,
        mesh=mesh,
        in_specs=(rows, rows, rows, rows, P("dp", "sp"), P(None, "dp"), rows),
        out_specs=(rows, rows, rows, rows),
        check_vma=False,
    )
```
